128 devices in a mesh: row: 8 (over z_lo, x), col: 16 (over z_hi, y, core).
Axes of the slice: x: 4, y: 4, z: 4 (z_hi: 2, z_lo: 2; z = z_hi * 2 + z_lo), core: 2. Of those that a mesh axis runs over, the one named last changes fastest.
Arguments:
- activations: bfloat16 [32768, 4096], P(('row', 'col')), may hold values from -6 to 6
- out_grads: bfloat16 [32768, 4096], P(('row', 'col')), may hold values from -6 to 6
- proj_act: bfloat16 [4096, 160], replicated, may hold values from -0.09375 to 0.09375
- proj_grad: bfloat16 [4096, 128], replicated, may hold values from -0.09375 to 0.09375
- damping: float32 [20480], replicated, may hold values from 0.3 to 3
Outputs:
- factored: float32 [20480, 20480], P('row', 'col')
The draws below stay inside these ranges and needn't reach their ends.
All inputs are finite; a program needn't handle non-finite values.
Results may differ from the reference program's by a relative error of at most 0.0003.
Values sent between devices are 32-bit elements; how exact they have to be, the bound alone decides.
No kernel may reach another device: no remote copies, remote signals or barrier semaphores. Data moves between devices by JAX's collectives and lax.ppermute only.
A program may use at most 192 MiB of HBM per device.

```python
import math
import jax
import jax.numpy as jnp
from jax import lax

D = 4096
SA = 160
SG = 128
TOK_EX = 64
B = 128
PW = 512
PANELS = 2
F = 20480
NEX = 512
TOKENS = 32768
N_ROW = 8
N_COL = 16


def level_of(rng, shape, shards, smallest, largest):
    gain = 1.0
    for dim, blocks in shards:
        steps = jax.random.uniform(jax.random.fold_in(jax.random.fold_in(rng, 6), dim), (blocks,), jnp.float32, smallest / len(shards), largest / len(shards))
        gain = gain * jnp.repeat(jnp.exp(steps), shape[dim] // blocks).reshape((-1,) + (1,) * (len(shape) - 1 - dim))
    return gain


def scatter_about(rng, extent, width, limit, shards=(), kind=jnp.bfloat16):
    gain = level_of(rng, extent, shards, -0.22, 0.18) if shards else 1.0
    entries = jax.random.normal(rng, extent, jnp.float32) * width * gain
    return jnp.minimum(jnp.maximum(entries, -limit), limit).astype(kind)


def setup_inputs(seed: int = 0) -> dict:
    key_list = jax.random.split(jax.random.key(seed), 6)
    return {
        "activations": scatter_about(key_list[0], (TOKENS, D), 1.0, 6.0, ((0, 128),)),
        "out_grads": scatter_about(key_list[1], (TOKENS, D), 1.0, 6.0, ((0, 128),)),
        "proj_act": scatter_about(key_list[2], (D, SA), D ** -0.5, 0.09375),
        "proj_grad": scatter_about(key_list[3], (D, SG), D ** -0.5, 0.09375),
        "damping": jnp.clip(jnp.exp(jax.random.uniform(key_list[4], (F,), jnp.float32, math.log(0.3), math.log(3.0))), 0.3, 3.0),
    }


def cyclic_map(total, groups):
    positions = jnp.arange(total, dtype=jnp.int32)
    per_group = total // groups
    inside = positions % per_group
    return (inside // B * groups + positions // per_group) * B + inside % B

def reference(activations, out_grads, proj_act, proj_grad, damping):
    act_sketch = jnp.dot(activations.astype(jnp.float32), proj_act.astype(jnp.float32), preferred_element_type=jnp.float32)
    grad_sketch = jnp.dot(out_grads.astype(jnp.float32), proj_grad.astype(jnp.float32), preferred_element_type=jnp.float32)
    sketches = jnp.einsum('eti,etj->eij', act_sketch.reshape(NEX, TOK_EX, SA), grad_sketch.reshape(NEX, TOK_EX, SG), precision=lax.Precision.HIGHEST) * TOK_EX ** (-0.5)
    sketches = sketches.reshape(NEX, F)
    curvature = lax.dot_general(sketches.astype(jnp.float32), sketches.astype(jnp.float32), (((0,), (0,)), ((), ())), precision=lax.Precision.HIGHEST, preferred_element_type=jnp.float32) / NEX
    curvature = curvature + jnp.diag(damping)
    row_ids = jnp.arange(F, dtype=jnp.int32)
    for panel_no in range(PANELS):
        first_col = panel_no * PW
        end_col = first_col + PW
        factor = jnp.linalg.cholesky(curvature[first_col:end_col, first_col:end_col])
        solved = jax.scipy.linalg.solve_triangular(factor, curvature[:, first_col:end_col].T, lower=True).T
        solved = jnp.where((row_ids >= first_col)[:, None], solved, 0.0)
        curvature = curvature.at[:, first_col:end_col].set(solved)
        tail_rows = solved[end_col:]
        update = lax.dot_general(tail_rows.astype(jnp.float32), tail_rows.astype(jnp.float32), (((1,), (1,)), ((), ())), precision=lax.Precision.HIGHEST, preferred_element_type=jnp.float32)
        curvature = curvature.at[end_col:, end_col:].add(-update)
    finished = PANELS * PW
    curvature = curvature.at[:finished, finished:].set(0.0)
    row_map = cyclic_map(F, N_ROW)
    col_map = cyclic_map(F, N_COL)
    return curvature[row_map][:, col_map]
```

```python
import functools

import jax
import jax.numpy as jnp
from jax import lax
from jax.experimental import pallas as pl
from jax.experimental.pallas import tpu as pltpu
from jax.sharding import PartitionSpec as P

SA = 160
SG = 128
TOK_EX = 64
B = 128
PW = 512
PANELS = 2
NEX = 512
F = SA * SG
N_ROW = 8
N_COL = 16
FINISHED = PW * PANELS
PANEL_BLOCKS = FINISHED // B

PRECISE = lax.Precision.HIGHEST


def contract(left, right, left_dim, right_dim):
    return lax.dot_general(
        left,
        right,
        (((left_dim,), (right_dim,)), ((), ())),
        precision=PRECISE,
        preferred_element_type=jnp.float32,
    )


def single(left, right):
    return jnp.dot(left, right, preferred_element_type=jnp.float32)


def halves(value):
    high = value.astype(jnp.bfloat16)
    return high, (value - high.astype(jnp.float32)).astype(jnp.bfloat16)


def eliminate(square):
    sub = lax.broadcasted_iota(jnp.int32, (8, B), 0)
    lane = lax.broadcasted_iota(jnp.int32, (8, B), 1)
    tiles = [square[8 * t : 8 * t + 8, :] for t in range(B // 8)]
    for group in range(B // 8):
        first = 8 * group
        cols = {}
        for t in range(group, B // 8):
            for w in range(8):
                cols[t, w] = jnp.broadcast_to(tiles[t][:, first + w : first + w + 1], (8, B))
        scale = None
        for w in range(8):
            here = lane == first + w
            pivot = jnp.broadcast_to(cols[group, w][w : w + 1, :], (8, B))
            later = [jnp.broadcast_to(cols[group, v][w : w + 1, :], (8, B)) for v in range(w + 1, 8)]
            inverse = 1.0 / pivot
            row = jnp.where(here, 1.0, jnp.broadcast_to(tiles[group][w : w + 1, :], (8, B)))
            for t in range(group, B // 8):
                column = cols[t, w]
                cleared = here
                if t == group:
                    column = jnp.where(sub > w, column, 0.0)
                    cleared = here & (sub > w)
                ratio = column * inverse
                for v in range(w + 1, 8):
                    cols[t, v] = cols[t, v] - ratio * later[v - w - 1]
                tiles[t] = jnp.where(cleared, 0.0, tiles[t]) - ratio * row
            root = lax.rsqrt(pivot)
            scale = root if scale is None else jnp.where(sub >= w, root, scale)
        tiles[group] = jnp.where(lane == sub + first, scale, tiles[group] * scale)
    lower = [jnp.where(lane <= sub + 8 * t, tile, 0.0) for t, tile in enumerate(tiles)]
    upper = [
        jnp.where(lane > sub + 8 * t, tile, jnp.where(lane == sub + 8 * t, 1.0 / tile, 0.0))
        for t, tile in enumerate(tiles)
    ]
    return jnp.concatenate(upper, 0), jnp.concatenate(lower, 0)


def chain_kernel(count, x_ref, xt_ref, damp_ref, start_ref, m_ref, y_ref, u_ref, s_ref, last_ref):
    down = lax.broadcasted_iota(jnp.int32, (B, B), 0)
    along = lax.broadcasted_iota(jnp.int32, (B, B), 1)

    def ridge(k):
        return jnp.where(down == along, jnp.broadcast_to(damp_ref[pl.ds(k, 1), :], (B, B)), 0.0)

    m_ref[...] = start_ref[...]
    last_ref[...] = jnp.zeros_like(last_ref)
    first = contract(start_ref[...], x_ref[:, :B], 1, 0)
    s_ref[...] = contract(xt_ref[:B, :], first, 1, 0) + ridge(0)

    def body(k, carry):
        here = pl.multiple_of(k * B, B)
        following = jnp.minimum(k + 1, count - 1)
        there = pl.multiple_of(following * B, B)
        square = s_ref[...]
        last = last_ref[...]
        m_now = m_ref[...] - contract(last, last, 1, 1)
        m_ref[...] = m_now
        pair = jnp.concatenate([x_ref[:, pl.ds(here, B)], x_ref[:, pl.ds(there, B)]], 1)
        both = contract(m_now, pair, 1, 0)
        ahead = contract(xt_ref[pl.ds(there, B), :], both, 1, 0)
        upper, inverse = eliminate(square)
        below = contract(ahead[:, :B], inverse, 1, 1)
        s_ref[...] = ahead[:, B:] - contract(below, below, 1, 1) + ridge(following)
        y_now = contract(both[:, :B], inverse, 1, 1)
        last_ref[...] = y_now
        y_ref[:, pl.ds(here, B)] = y_now
        u_ref[pl.ds(here, B), :] = upper
        return carry

    lax.fori_loop(0, count, body, 0)
    last = last_ref[...]
    m_ref[...] = m_ref[...] - contract(last, last, 1, 1)


def chain(x, xt, damp, start):
    count = x.shape[1] // B
    return pl.pallas_call(
        functools.partial(chain_kernel, count),
        out_shape=(
            jax.ShapeDtypeStruct((NEX, NEX), jnp.float32),
            jax.ShapeDtypeStruct((NEX, count * B), jnp.float32),
            jax.ShapeDtypeStruct((count * B, B), jnp.float32),
        ),
        scratch_shapes=[pltpu.VMEM((B, B), jnp.float32), pltpu.VMEM((NEX, B), jnp.float32)],
        compiler_params=pltpu.CompilerParams(vmem_limit_bytes=24 << 20),
        cost_estimate=pl.CostEstimate(flops=20_000_000_000, bytes_accessed=120_000_000, transcendentals=0),
        name="chain",
    )(x, xt, damp, start)


def tile_kernel(
    place_ref, xr_ref, xc_ref, m_ref, y_ref, u_ref, damp_ref, mid_col, mid_row, row_col, col_row, out_ref, high_ref, low_ref
):
    step = pl.program_id(0)
    row_index = place_ref[0]
    col_index = place_ref[1]
    cols_here = xc_ref.shape[1]
    has_panel = col_index < PANEL_BLOCKS

    @pl.when(step == 0)
    def _():
        to_rows = jnp.where(row_col[...] == mid_row[...], 1.0, 0.0).astype(jnp.bfloat16)
        to_cols = jnp.where(mid_col[...] == col_row[...], 1.0, 0.0).astype(jnp.bfloat16)
        m_parts = []
        for part in halves(m_ref[...]):
            turned = single(to_rows, part).astype(jnp.bfloat16)
            m_parts.append(single(turned, to_cols).astype(jnp.bfloat16))
        for start in range(0, cols_here, 256):
            x_high, x_low = halves(xc_ref[:, start : start + 256])
            right = single(m_parts[0], x_high) + single(m_parts[0], x_low) + single(m_parts[1], x_high)
            high, low = halves(right)
            high_ref[:, start : start + 256] = high
            low_ref[:, start : start + 256] = low

        @pl.when(has_panel)
        def _():
            at = pl.multiple_of(jnp.minimum(col_index, PANEL_BLOCKS - 1) * B, B)
            y_high, y_low = halves(y_ref[:, pl.ds(at, B)])
            high_ref[:, :B] = single(to_rows, y_high).astype(jnp.bfloat16)
            low_ref[:, :B] = single(to_rows, y_low).astype(jnp.bfloat16)

    left_high, left_low = halves(xr_ref[...].T)
    for start in range(0, cols_here, 256):
        high = high_ref[:, start : start + 256]
        low = low_ref[:, start : start + 256]
        out_ref[:, start : start + 256] = single(left_high, high) + single(left_high, low) + single(left_low, high)

    down = lax.broadcasted_iota(jnp.int32, (B, B), 0)
    along = lax.broadcasted_iota(jnp.int32, (B, B), 1)

    @pl.when(row_index == col_index % N_ROW)
    def _():
        upper_half = col_index // N_ROW
        rows = pl.ds(pl.multiple_of(upper_half * B, B), B)
        cols = pl.ds(pl.multiple_of(step * B, B), B)
        ridge = jnp.broadcast_to(damp_ref[pl.ds(col_index + N_COL * step, 1), :], (B, B))
        out_ref[rows, cols] = out_ref[rows, cols] + jnp.where(down == along, ridge, 0.0)

    @pl.when(step == 0)
    def _():
        product = out_ref[:B, :B]
        out_ref[:B, :] = jnp.zeros((B, cols_here), jnp.float32)

        @pl.when(has_panel & (row_index > col_index))
        def _():
            out_ref[:B, :B] = product

        @pl.when(has_panel & (row_index == col_index))
        def _():
            at = pl.multiple_of(jnp.minimum(col_index, PANEL_BLOCKS - 1) * B, B)
            out_ref[:B, :B] = u_ref[pl.ds(at, B), :].T


def tile(place, xr, xc, m, y, u, damp, mid, row, col):
    rows_here = xr.shape[1]
    cols_here = xc.shape[1]

    def whole(shape):
        return pl.BlockSpec(shape, lambda i: (0, 0))

    return pl.pallas_call(
        tile_kernel,
        grid=(rows_here // 256,),
        out_shape=jax.ShapeDtypeStruct((rows_here, cols_here), jnp.float32),
        in_specs=[
            pl.BlockSpec(memory_space=pltpu.SMEM),
            pl.BlockSpec((NEX, 256), lambda i: (0, i)),
            whole(xc.shape),
            whole(m.shape),
            whole(y.shape),
            whole(u.shape),
            whole(damp.shape),
            whole((NEX, 1)),
            whole((1, NEX)),
            whole((NEX, 1)),
            whole((1, NEX)),
        ],
        out_specs=pl.BlockSpec((256, cols_here), lambda i: (i, 0)),
        scratch_shapes=[pltpu.VMEM((NEX, cols_here), jnp.bfloat16)] * 2,
        compiler_params=pltpu.CompilerParams(vmem_limit_bytes=40 << 20),
        cost_estimate=pl.CostEstimate(flops=12_000_000_000, bytes_accessed=24_000_000, transcendentals=0),
        name="tile",
    )(
        place, xr, xc, m, y, u, damp, mid.reshape(-1, 1), mid.reshape(1, -1), row.reshape(-1, 1), col.reshape(1, -1)
    )


def swap(value, mask):
    devices = N_ROW * N_COL
    return lax.ppermute(value, ("row", "col"), [(i, i ^ mask) for i in range(devices)])


ROW_LOW, ROW_HIGH = (16, 32, 48), (64,)
COL_CORE, COL_LOW, COL_HIGH = (1,), (2, 4, 6), (8,)


def spread_out(value, phases):
    masks = [0]
    for phase in phases:
        value = jnp.concatenate([value] + [swap(value, mask) for mask in phase], 0)
        masks = [held ^ mask for mask in (0,) + phase for held in masks]
    return value, masks


def shards(activations, out_grads, proj_act, proj_grad, damping):
    row_index = lax.axis_index("row")
    col_index = lax.axis_index("col")
    me = row_index * N_COL + col_index
    act_sketch = jnp.dot(activations, proj_act, preferred_element_type=jnp.float32)
    grad_sketch = jnp.dot(out_grads, proj_grad, preferred_element_type=jnp.float32)
    here = activations.shape[0] // TOK_EX
    sketches = jnp.einsum(
        "eti,etj->eij",
        act_sketch.reshape(here, TOK_EX, SA),
        grad_sketch.reshape(here, TOK_EX, SG),
        precision=PRECISE,
    ) * (TOK_EX * NEX) ** (-0.5)
    sketches = sketches.reshape(here, F)
    rows_here = F // N_ROW
    cols_here = F // N_COL

    x_panel, masks = spread_out(sketches[:, :FINISHED], (ROW_LOW, ROW_HIGH, COL_HIGH, COL_LOW, COL_CORE))
    examples = jnp.arange(here, dtype=jnp.int32)
    mid_ids = ((me ^ jnp.array(masks, jnp.int32))[:, None] * here + examples).reshape(-1)

    by_rows = lax.all_to_all(
        sketches.reshape(here, rows_here // B, N_ROW, B), "row", split_axis=2, concat_axis=0, tiled=True
    ).reshape(N_ROW * here, rows_here)
    by_cols = lax.all_to_all(
        sketches.reshape(here, cols_here // B, N_COL, B), "col", split_axis=2, concat_axis=0, tiled=True
    ).reshape(N_COL * here, cols_here)
    xr = lax.all_gather(by_rows, "col", axis=0, tiled=True)
    xc = lax.all_gather(by_cols, "row", axis=0, tiled=True)
    positions = jnp.arange(N_ROW * N_COL, dtype=jnp.int32)
    col_ids = (positions[:, None] * here + examples).reshape(-1)
    row_ids = ((positions % N_ROW * N_COL + positions // N_ROW)[:, None] * here + examples).reshape(-1)

    damp_blocks = damping.reshape(F // B, B)
    m, y, u = chain(x_panel, x_panel.T, damp_blocks[:PANEL_BLOCKS], jnp.eye(NEX, dtype=jnp.float32))
    place = jnp.stack([row_index, col_index]).astype(jnp.int32)
    return tile(place, xr, xc, m, y, u, damp_blocks, mid_ids, row_ids, col_ids)


def solution(mesh):
    placed = (P(("row", "col"), None), P(("row", "col"), None), P(), P(), P())
    return jax.shard_map(
        shards, mesh=mesh, in_specs=placed, out_specs=P("row", "col"), check_vma=False
    )
```

```python
import functools

import jax
import jax.numpy as jnp
from jax import lax
from jax.experimental import pallas as pl
from jax.experimental.pallas import tpu as pltpu
from jax.sharding import PartitionSpec as P

SA = 160
SG = 128
TOK_EX = 64
B = 128
PW = 512
PANELS = 2
NEX = 512
F = SA * SG
N_ROW = 8
N_COL = 16
FINISHED = PW * PANELS
PANEL_BLOCKS = FINISHED // B
CALLS = (2, 3, 3)
VMEM = 60 << 20
ROW_BLOCKS = SA // N_ROW
COL_BLOCKS = SA // N_COL

PRECISE = lax.Precision.HIGHEST


def contract(left, right, left_dim, right_dim):
    return lax.dot_general(
        left,
        right,
        (((left_dim,), (right_dim,)), ((), ())),
        precision=PRECISE,
        preferred_element_type=jnp.float32,
    )


def single(left, right):
    return jnp.dot(left, right, preferred_element_type=jnp.float32)


def halves(value):
    high = value.astype(jnp.bfloat16)
    return high, (value - high.astype(jnp.float32)).astype(jnp.bfloat16)


def eliminate(square):
    sub = lax.broadcasted_iota(jnp.int32, (8, B), 0)
    lane = lax.broadcasted_iota(jnp.int32, (8, B), 1)
    tiles = [square[8 * t : 8 * t + 8, :] for t in range(B // 8)]
    for group in range(B // 8):
        first = 8 * group
        cols = {}
        for t in range(group, B // 8):
            for w in range(8):
                cols[t, w] = jnp.broadcast_to(tiles[t][:, first + w : first + w + 1], (8, B))
        scale = None
        for w in range(8):
            here = lane == first + w
            pivot = jnp.broadcast_to(cols[group, w][w : w + 1, :], (8, B))
            later = [jnp.broadcast_to(cols[group, v][w : w + 1, :], (8, B)) for v in range(w + 1, 8)]
            inverse = 1.0 / pivot
            row = jnp.where(here, 1.0, jnp.broadcast_to(tiles[group][w : w + 1, :], (8, B)))
            for t in range(group, B // 8):
                column = cols[t, w]
                cleared = here
                if t == group:
                    column = jnp.where(sub > w, column, 0.0)
                    cleared = here & (sub > w)
                ratio = column * inverse
                for v in range(w + 1, 8):
                    cols[t, v] = cols[t, v] - ratio * later[v - w - 1]
                tiles[t] = jnp.where(cleared, 0.0, tiles[t]) - ratio * row
            root = lax.rsqrt(pivot)
            scale = root if scale is None else jnp.where(sub >= w, root, scale)
        tiles[group] = jnp.where(lane == sub + first, scale, tiles[group] * scale)
    lower = [jnp.where(lane <= sub + 8 * t, tile, 0.0) for t, tile in enumerate(tiles)]
    upper = [
        jnp.where(lane > sub + 8 * t, tile, jnp.where(lane == sub + 8 * t, 1.0 / tile, 0.0))
        for t, tile in enumerate(tiles)
    ]
    return jnp.concatenate(upper, 0), jnp.concatenate(lower, 0)


def chain_kernel(first_block, count, pieces, *refs):
    x_refs, refs = refs[:pieces], refs[pieces:]
    if first_block == 0:
        damp_ref, m_ref, y_ref, u_ref, s_ref, last_ref = refs
    else:
        damp_ref, start_ref, m_ref, y_ref, u_ref, s_ref, last_ref = refs
    down = lax.broadcasted_iota(jnp.int32, (B, B), 0)
    along = lax.broadcasted_iota(jnp.int32, (B, B), 1)

    def ridge(k):
        return jnp.where(down == along, jnp.broadcast_to(damp_ref[pl.ds(k, 1), :], (B, B)), 0.0)

    def columns(k):
        return jnp.concatenate([ref[k] for ref in x_refs], 0)

    block = columns(first_block)
    if first_block == 0:
        one = lax.broadcasted_iota(jnp.int32, (NEX, NEX), 0) == lax.broadcasted_iota(jnp.int32, (NEX, NEX), 1)
        m_ref[...] = jnp.where(one, 1.0, 0.0)
        s_ref[...] = contract(block.T, block, 1, 0) + ridge(first_block)
    else:
        m_ref[...] = start_ref[...]
        s_ref[...] = contract(block.T, contract(start_ref[...], block, 1, 0), 1, 0) + ridge(first_block)
    last_ref[...] = jnp.zeros_like(last_ref)

    def body(k, carry):
        here = first_block + k
        there = first_block + jnp.minimum(k + 1, count - 1)
        square = s_ref[...]
        last = last_ref[...]
        m_now = m_ref[...] - contract(last, last, 1, 1)
        m_ref[...] = m_now
        following = columns(there)
        both = contract(m_now, jnp.concatenate([columns(here), following], 1), 1, 0)
        ahead = contract(following.T, both, 1, 0)
        upper, inverse = eliminate(square)
        below = contract(ahead[:, :B], inverse, 1, 1)
        s_ref[...] = ahead[:, B:] - contract(below, below, 1, 1) + ridge(there)
        y_now = contract(both[:, :B], inverse, 1, 1)
        last_ref[...] = y_now
        y_ref[k] = y_now
        u_ref[k] = upper
        return carry

    lax.fori_loop(0, count, body, 0)
    last = last_ref[...]
    m_ref[...] = m_ref[...] - contract(last, last, 1, 1)


def chain(x, damp, first_block, count, start):
    return pl.pallas_call(
        functools.partial(chain_kernel, first_block, count, len(x)),
        out_shape=(
            jax.ShapeDtypeStruct((NEX, NEX), jnp.float32),
            jax.ShapeDtypeStruct((count, NEX, B), jnp.float32),
            jax.ShapeDtypeStruct((count, B, B), jnp.float32),
        ),
        scratch_shapes=[pltpu.VMEM((B, B), jnp.float32), pltpu.VMEM((NEX, B), jnp.float32)],
        compiler_params=pltpu.CompilerParams(vmem_limit_bytes=VMEM),
        cost_estimate=pl.CostEstimate(flops=6_000_000_000 * count, bytes_accessed=16_000_000 * count, transcendentals=0),
        name="chain",
    )(*x, damp, *(() if start is None else (start,)))


def tile_kernel(place_ref, *refs):
    xr_refs = refs[:8]
    xc_ref, m_ref = refs[8:10]
    y_refs, u_refs = refs[10 : 10 + len(CALLS)], refs[10 + len(CALLS) : 10 + 2 * len(CALLS)]
    damp_ref, row_ids, col_ids, out_ref, high_ref, low_ref = refs[10 + 2 * len(CALLS) :]
    step = pl.program_id(0)
    row_index = place_ref[0]
    col_index = place_ref[1]
    cols_here = out_ref.shape[1]
    starts = [sum(CALLS[:call]) for call in range(len(CALLS))]
    in_call = [jnp.clip(col_index - start, 0, count - 1) for start, count in zip(starts, CALLS)]
    chosen = [(col_index >= start) & (col_index < start + count) for start, count in zip(starts, CALLS)]

    @pl.when(step == 0)
    def _():
        to_cols = jnp.where(row_ids[...] == col_ids[...], 1.0, 0.0).astype(jnp.bfloat16)
        m_high, m_low = [single(part, to_cols).astype(jnp.bfloat16) for part in halves(m_ref[...])]
        for start in range(0, COL_BLOCKS, 2):
            columns = [
                jnp.concatenate([xc_ref[piece, start + k] for piece in range(xc_ref.shape[0])], 0) for k in range(2)
            ]
            x_high, x_low = halves(jnp.concatenate(columns, 1))
            right = single(m_high, x_high) + single(m_high, x_low) + single(m_low, x_high)
            high, low = halves(right)
            high_ref[:, start * B : (start + 2) * B] = high
            low_ref[:, start * B : (start + 2) * B] = low

        for call, y_ref in enumerate(y_refs):

            @pl.when(chosen[call])
            def _(call=call, y_ref=y_ref):
                high, low = halves(y_ref[in_call[call]])
                high_ref[:, :B] = high
                low_ref[:, :B] = low

    left = jnp.concatenate([jnp.concatenate([ref[k] for ref in xr_refs], 0).T for k in range(2)], 0)
    left_high, left_low = halves(left)
    for start in range(0, cols_here, 256):
        high = high_ref[:, start : start + 256]
        low = low_ref[:, start : start + 256]
        out_ref[:, start : start + 256] = single(left_high, high) + single(left_high, low) + single(left_low, high)

    down = lax.broadcasted_iota(jnp.int32, (B, B), 0)
    along = lax.broadcasted_iota(jnp.int32, (B, B), 1)

    @pl.when(row_index == col_index % N_ROW)
    def _():
        rows = pl.ds(pl.multiple_of(col_index // N_ROW * B, B), B)
        cols = pl.ds(pl.multiple_of(step * B, B), B)
        ridge = jnp.broadcast_to(damp_ref[pl.ds(col_index + N_COL * step, 1), :], (B, B))
        out_ref[rows, cols] = out_ref[rows, cols] + jnp.where(down == along, ridge, 0.0)

    @pl.when(step == 0)
    def _():
        product = out_ref[:B, :B]
        out_ref[:B, :] = jnp.zeros((B, cols_here), jnp.float32)

        @pl.when((col_index < PANEL_BLOCKS) & (row_index > col_index))
        def _():
            out_ref[:B, :B] = product

        for call, u_ref in enumerate(u_refs):

            @pl.when(chosen[call] & (row_index == col_index))
            def _(call=call, u_ref=u_ref):
                out_ref[:B, :B] = u_ref[in_call[call]].T


def tile(place, xr, xc, m, y, u, damp, row_ids, col_ids):
    rows_here, cols_here = ROW_BLOCKS * B, COL_BLOCKS * B

    def whole(value):
        return pl.BlockSpec(value.shape, lambda i: (0,) * value.ndim)

    rest = (xc, m, *y, *u, damp, row_ids.reshape(-1, 1), col_ids.reshape(1, -1))
    return pl.pallas_call(
        tile_kernel,
        grid=(ROW_BLOCKS // 2,),
        out_shape=jax.ShapeDtypeStruct((rows_here, cols_here), jnp.float32),
        in_specs=[pl.BlockSpec(memory_space=pltpu.SMEM)]
        + [pl.BlockSpec((2,) + piece.shape[1:], lambda i: (i, 0, 0)) for piece in xr]
        + [whole(value) for value in rest],
        out_specs=pl.BlockSpec((2 * B, cols_here), lambda i: (i, 0)),
        scratch_shapes=[pltpu.VMEM((NEX, cols_here), jnp.bfloat16)] * 2,
        compiler_params=pltpu.CompilerParams(vmem_limit_bytes=VMEM),
        cost_estimate=pl.CostEstimate(flops=12_000_000_000, bytes_accessed=24_000_000, transcendentals=0),
        name="tile",
    )(place, *xr, *rest)


def moved(value, target):
    pairs = [(row * N_COL + col, target(row, col)) for row in range(N_ROW) for col in range(N_COL)]
    return lax.ppermute(value, ("row", "col"), pairs)


def swapped(value, mask):
    return moved(value, lambda row, col: row * N_COL + (col ^ mask))


FAR, RING, CORE = 8, (2, 4, 6), 1


def shards(activations, out_grads, proj_act, proj_grad, damping):
    row_index = lax.axis_index("row")
    col_index = lax.axis_index("col")
    act_sketch = jnp.dot(activations, proj_act, preferred_element_type=jnp.float32)
    grad_sketch = jnp.dot(out_grads, proj_grad, preferred_element_type=jnp.float32)
    here = activations.shape[0] // TOK_EX
    sketches = jnp.einsum(
        "eti,etj->eij",
        act_sketch.reshape(here, TOK_EX, SA),
        grad_sketch.reshape(here, TOK_EX, SG),
        precision=PRECISE,
    ) * (TOK_EX * NEX) ** (-0.5)

    for_rows = sketches.reshape(here, ROW_BLOCKS, N_ROW, B).transpose(2, 1, 0, 3)
    for_panel = jnp.broadcast_to(
        sketches[:, :PANEL_BLOCKS].transpose(1, 0, 2), (N_ROW, PANEL_BLOCKS, here, B)
    )
    parcels = lax.all_to_all(jnp.concatenate([for_rows, for_panel], 1), "row", split_axis=0, concat_axis=0)
    group = N_ROW * here
    parcels = parcels.transpose(1, 0, 2, 3).reshape(ROW_BLOCKS + PANEL_BLOCKS, group, B)
    rows = parcels[:ROW_BLOCKS]
    panel = parcels[ROW_BLOCKS:]

    parity = col_index % 2
    split = rows.reshape(COL_BLOCKS, 2, group, B)
    near = lax.dynamic_index_in_dim(split, parity, 1, keepdims=False)
    other = lax.dynamic_index_in_dim(split, 1 - parity, 1, keepdims=False)
    panel_far = swapped(panel, FAR)
    near = moved(near, lambda row, col: col // 2 * N_COL + row + N_ROW * (col % 2))
    other = moved(other, lambda row, col: col // 2 * N_COL + row + N_ROW * (1 - col % 2))
    rows_far = swapped(rows, FAR)
    panel = jnp.concatenate([panel, panel_far], 1)
    panels = [panel] + [swapped(panel, mask) for mask in RING]
    panels = panels + [swapped(piece, CORE) for piece in panels]

    damp_blocks = damping.reshape(SA, B)
    m, y0, u0 = chain(panels, damp_blocks, 0, CALLS[0], None)
    m, near, other, rows, rows_far = lax.optimization_barrier((m, near, other, rows, rows_far))
    xc = lax.all_gather(jnp.concatenate([near, other], 1), "row", axis=0)
    rows = jnp.concatenate([rows, rows_far], 1)
    pieces = [rows] + [swapped(rows, mask) for mask in RING]
    m, y1, u1 = chain(panels, damp_blocks, CALLS[0], CALLS[1], m)
    m, pieces = lax.optimization_barrier((m, pieces))
    pieces = pieces + [swapped(piece, CORE) for piece in pieces]
    m, y2, u2 = chain(panels, damp_blocks, CALLS[0] + CALLS[1], CALLS[2], m)

    ex = jnp.arange(here, dtype=jnp.int32)
    line = jnp.arange(N_ROW, dtype=jnp.int32)[:, None] * N_COL
    masks = [core ^ ring ^ far for core in (0, CORE) for ring in (0,) + RING for far in (0, FAR)]
    row_ids = (line + (col_index ^ jnp.array(masks, jnp.int32))[:, None, None])[..., None] * here + ex
    turn = col_index // N_ROW ^ jnp.arange(2, dtype=jnp.int32)
    sources = 2 * jnp.arange(N_ROW, dtype=jnp.int32)[:, None] + turn
    col_ids = (line + sources[:, :, None, None])[..., None] * here + ex
    place = jnp.stack([row_index, col_index]).astype(jnp.int32)
    return tile(place, pieces, xc, m, (y0, y1, y2), (u0, u1, u2), damp_blocks, row_ids.reshape(-1), col_ids.reshape(-1))


def solution(mesh):
    placed = (P(("row", "col"), None), P(("row", "col"), None), P(), P(), P())
    return jax.shard_map(
        shards, mesh=mesh, in_specs=placed, out_specs=P("row", "col"), check_vma=False
    )
```

```python
import functools

import jax
import jax.numpy as jnp
from jax import lax
from jax.experimental import pallas as pl
from jax.experimental.pallas import tpu as pltpu
from jax.sharding import PartitionSpec as P

SA = 160
SG = 128
TOK_EX = 64
B = 128
PW = 512
PANELS = 2
NEX = 512
F = SA * SG
N_ROW = 8
N_COL = 16
FINISHED = PW * PANELS
PANEL_BLOCKS = FINISHED // B
CALLS = (2, 2, 2, 2)
FIRSTS = (0, 2, 4, 6)
STEP_BLOCKS = 4
CHAIN_VMEM = 24 << 20
TILE_VMEM = 32 << 20
ROW_BLOCKS = SA // N_ROW
COL_BLOCKS = SA // N_COL

PRECISE = lax.Precision.HIGHEST


def contract(left, right, left_dim, right_dim):
    return lax.dot_general(
        left,
        right,
        (((left_dim,), (right_dim,)), ((), ())),
        precision=PRECISE,
        preferred_element_type=jnp.float32,
    )


def single(left, right):
    return jnp.dot(left, right, preferred_element_type=jnp.float32)


def halves(value):
    high = value.astype(jnp.bfloat16)
    return high, (value - high.astype(jnp.float32)).astype(jnp.bfloat16)


def eliminate(square):
    sub = lax.broadcasted_iota(jnp.int32, (8, B), 0)
    lane = lax.broadcasted_iota(jnp.int32, (8, B), 1)
    tiles = [square[8 * t : 8 * t + 8, :] for t in range(B // 8)]
    for group in range(B // 8):
        first = 8 * group
        cols = {}
        for t in range(group, B // 8):
            for w in range(8):
                cols[t, w] = jnp.broadcast_to(tiles[t][:, first + w : first + w + 1], (8, B))
        scale = None
        for w in range(8):
            here = lane == first + w
            pivot = jnp.broadcast_to(cols[group, w][w : w + 1, :], (8, B))
            later = [jnp.broadcast_to(cols[group, v][w : w + 1, :], (8, B)) for v in range(w + 1, 8)]
            inverse = 1.0 / pivot
            row = jnp.where(here, 1.0, jnp.broadcast_to(tiles[group][w : w + 1, :], (8, B)))
            for t in range(group, B // 8):
                column = cols[t, w]
                cleared = here
                if t == group:
                    column = jnp.where(sub > w, column, 0.0)
                    cleared = here & (sub > w)
                ratio = column * inverse
                for v in range(w + 1, 8):
                    cols[t, v] = cols[t, v] - ratio * later[v - w - 1]
                tiles[t] = jnp.where(cleared, 0.0, tiles[t]) - ratio * row
            root = lax.rsqrt(pivot)
            scale = root if scale is None else jnp.where(sub >= w, root, scale)
        tiles[group] = jnp.where(lane == sub + first, scale, tiles[group] * scale)
    lower = [jnp.where(lane <= sub + 8 * t, tile, 0.0) for t, tile in enumerate(tiles)]
    upper = [
        jnp.where(lane > sub + 8 * t, tile, jnp.where(lane == sub + 8 * t, 1.0 / tile, 0.0))
        for t, tile in enumerate(tiles)
    ]
    return jnp.concatenate(upper, 0), jnp.concatenate(lower, 0)


def chain_kernel(call, pieces, *refs):
    first = call == 0
    final = call == len(CALLS) - 1
    count = CALLS[call]
    x_refs, refs = refs[:pieces], refs[pieces:]
    after_refs = ()
    if not final:
        after_refs, refs = refs[:pieces], refs[pieces:]
    if first:
        damp_ref, m_ref, y_ref, u_ref, s_ref, x_ref, last_ref = refs
    else:
        damp_ref, start_ref, square_ref, before_ref, m_ref, y_ref, u_ref, s_ref, x_ref, last_ref = refs
    ahead_last = count - 1 if final else count
    first_block = FIRSTS[call]
    down = lax.broadcasted_iota(jnp.int32, (B, B), 0)
    along = lax.broadcasted_iota(jnp.int32, (B, B), 1)

    def ridge(k):
        return jnp.where(down == along, jnp.broadcast_to(damp_ref[pl.ds(k, 1), :], (B, B)), 0.0)

    for k in range(count):
        x_ref[k] = jnp.concatenate([ref[k] for ref in x_refs], 0)
    if not final:
        x_ref[count] = jnp.concatenate([ref[0] for ref in after_refs], 0)
    if first:
        one = lax.broadcasted_iota(jnp.int32, (NEX, NEX), 0) == lax.broadcasted_iota(jnp.int32, (NEX, NEX), 1)
        m_ref[...] = jnp.where(one, 1.0, 0.0)
        block = x_ref[0]
        s_ref[...] = contract(block.T, block, 1, 0) + ridge(0)
        last_ref[...] = jnp.zeros_like(last_ref)
    else:
        m_ref[...] = start_ref[...]
        s_ref[...] = square_ref[...]
        last_ref[...] = before_ref[0]

    def body(k, carry):
        there = jnp.minimum(k + 1, ahead_last)
        square = s_ref[...]
        last = last_ref[...]
        m_now = m_ref[...] - contract(last, last, 1, 1)
        m_ref[...] = m_now
        following = x_ref[there]
        both = contract(m_now, jnp.concatenate([x_ref[k], following], 1), 1, 0)
        ahead = contract(following.T, both, 1, 0)
        upper, inverse = eliminate(square)
        below = contract(ahead[:, :B], inverse, 1, 1)
        s_ref[...] = ahead[:, B:] - contract(below, below, 1, 1) + ridge(first_block + there)
        y_now = contract(both[:, :B], inverse, 1, 1)
        last_ref[...] = y_now
        y_ref[k] = y_now
        u_ref[k] = upper
        return carry

    lax.fori_loop(0, count, body, 0)
    if final:
        last = last_ref[...]
        m_ref[...] = m_ref[...] - contract(last, last, 1, 1)


def chain(x, damp, call, state):
    first = call == 0
    final = call == len(CALLS) - 1
    count = CALLS[call]
    operands = list(x)
    specs = [pl.BlockSpec((count,) + piece.shape[1:], lambda i: (FIRSTS[call] // count, 0, 0)) for piece in x]
    if not final:
        operands += x
        specs += [pl.BlockSpec((1,) + piece.shape[1:], lambda i: (FIRSTS[call + 1], 0, 0)) for piece in x]
    operands.append(damp)
    specs.append(pl.BlockSpec(damp.shape, lambda i: (0, 0)))
    if not first:
        operands += state
        specs += [
            pl.BlockSpec((NEX, NEX), lambda i: (0, 0)),
            pl.BlockSpec((B, B), lambda i: (0, 0)),
            pl.BlockSpec((1, NEX, B), lambda i: (CALLS[call - 1] - 1, 0, 0)),
        ]
    shapes = ((NEX, NEX), (count, NEX, B), (count, B, B), (B, B))
    return pl.pallas_call(
        functools.partial(chain_kernel, call, len(x)),
        grid=(1,),
        in_specs=specs,
        out_specs=tuple(pl.BlockSpec(shape, lambda i, rank=len(shape): (0,) * rank) for shape in shapes),
        out_shape=tuple(jax.ShapeDtypeStruct(shape, jnp.float32) for shape in shapes),
        scratch_shapes=[
            pltpu.VMEM((count + 1, NEX, B), jnp.float32),
            pltpu.VMEM((NEX, B), jnp.float32),
        ],
        compiler_params=pltpu.CompilerParams(vmem_limit_bytes=CHAIN_VMEM),
        cost_estimate=pl.CostEstimate(
            flops=6_000_000_000 * count, bytes_accessed=16_000_000 * count, transcendentals=0
        ),
        name="chain",
    )(*operands)


def example_ids(row_index, col_index):
    at = lax.broadcasted_iota(jnp.int32, (NEX, 1), 0)
    mask = (at >> 8 & 1) * CORE + (at >> 6 & 3) * RING[0] + (at >> 5 & 1) * FAR
    row_ids = ((at >> 2 & 7) * N_COL + (col_index ^ mask)) * 4 + (at & 3)
    at = lax.broadcasted_iota(jnp.int32, (1, NEX), 1)
    source = row_index ^ (at >> 7 & 3) ^ (at >> 6 & 1) * NEXT
    half = jnp.where(col_index >= N_ROW, 1, 0) ^ (at >> 5 & 1)
    col_ids = ((at >> 2 & 7) * N_COL + 2 * source + half) * 4 + (at & 3)
    return row_ids, col_ids


def tile_kernel(row_pieces, col_pieces, *refs):
    xr_refs, refs = refs[:row_pieces], refs[row_pieces:]
    xc_refs, refs = refs[:col_pieces], refs[col_pieces:]
    calls = len(CALLS)
    y_refs, refs = refs[:calls], refs[calls:]
    u_refs, refs = refs[:calls], refs[calls:]
    m_ref, damp_ref, out_ref, high_ref, low_ref, xc_own, m_own, y_own, u_own, sems = refs[:10]
    lefts = (refs[10:12], refs[12:14])
    step = pl.program_id(0)
    row_index = lax.axis_index("row")
    col_index = lax.axis_index("col")
    cols_here = out_ref.shape[1]
    chosen = [(col_index >= first) & (col_index < first + count) for first, count in zip(FIRSTS, CALLS)]
    in_call = [jnp.clip(col_index - first, 0, count - 1) for first, count in zip(FIRSTS, CALLS)]

    def m_copy():
        return pltpu.make_async_copy(m_ref, m_own, sems.at[0])

    def xc_copy(piece):
        return pltpu.make_async_copy(xc_refs[piece], xc_own.at[piece], sems.at[3 + piece])

    def y_copy(call):
        return pltpu.make_async_copy(y_refs[call].at[in_call[call]], y_own, sems.at[1])

    def u_copy(call):
        return pltpu.make_async_copy(u_refs[call].at[in_call[call]], u_own, sems.at[2])

    def turn(slot):
        for k in range(STEP_BLOCKS):
            left = jnp.concatenate([ref[k] for ref in xr_refs], 0).T
            for ref, part in zip(lefts[slot], halves(left)):
                ref[k * B : (k + 1) * B, :] = part

    def multiply(slot):
        for top in range(0, STEP_BLOCKS * B, 256):
            left_high = lefts[slot][0][top : top + 256, :]
            left_low = lefts[slot][1][top : top + 256, :]
            for start in range(0, cols_here, 256):
                high = high_ref[:, start : start + 256]
                low = low_ref[:, start : start + 256]
                out_ref[top : top + 256, start : start + 256] = (
                    single(left_high, high) + single(left_high, low) + single(left_low, high)
                )

    @pl.when(step == 0)
    def _():
        m_copy().start()
        for piece in range(col_pieces):
            xc_copy(piece).start()
        for call in range(calls):

            @pl.when(chosen[call])
            def _(call=call):
                y_copy(call).start()

            @pl.when(chosen[call] & (row_index == col_index))
            def _(call=call):
                u_copy(call).start()

        row_ids, col_ids = example_ids(row_index, col_index)
        to_cols = jnp.where(row_ids == col_ids, 1.0, 0.0).astype(jnp.bfloat16)
        turn(0)
        m_copy().wait()
        m_high, m_low = [single(part, to_cols).astype(jnp.bfloat16) for part in halves(m_own[...])]
        for piece in range(col_pieces):
            xc_copy(piece).wait()
        for start in range(0, COL_BLOCKS, 2):
            columns = [jnp.concatenate([xc_own[piece, start + k] for piece in range(col_pieces)], 0) for k in range(2)]
            x_high, x_low = halves(jnp.concatenate(columns, 1))
            right = single(m_high, x_high) + single(m_high, x_low) + single(m_low, x_high)
            high, low = halves(right)
            high_ref[:, start * B : (start + 2) * B] = high
            low_ref[:, start * B : (start + 2) * B] = low

        for call in range(calls):

            @pl.when(chosen[call])
            def _(call=call):
                y_copy(call).wait()
                high, low = halves(y_own[...])
                high_ref[:, :B] = high
                low_ref[:, :B] = low

            @pl.when(chosen[call] & (row_index == col_index))
            def _(call=call):
                u_copy(call).wait()

    for slot in range(2):

        @pl.when((step > 0) & ((step + 1) % 2 == slot))
        def _(slot=slot):
            multiply(slot)
            turn(1 - slot)

    @pl.when((step > 0) & (row_index == col_index % N_ROW))
    def _():
        down = lax.broadcasted_iota(jnp.int32, (B, B), 0)
        along = lax.broadcasted_iota(jnp.int32, (B, B), 1)
        upper_half = col_index // N_ROW
        for k in range(STEP_BLOCKS // 2):
            block = (step - 1) * (STEP_BLOCKS // 2) + k
            rows = pl.ds(pl.multiple_of((2 * k + upper_half) * B, B), B)
            cols = pl.ds(pl.multiple_of(block * B, B), B)
            ridge = jnp.broadcast_to(damp_ref[pl.ds(col_index + N_COL * block, 1), :], (B, B))
            out_ref[rows, cols] = out_ref[rows, cols] + jnp.where(down == along, ridge, 0.0)

    @pl.when(step == 1)
    def _():
        product = out_ref[:B, :B]
        out_ref[:B, :] = jnp.zeros((B, cols_here), jnp.float32)

        @pl.when((col_index < PANEL_BLOCKS) & (row_index > col_index))
        def _():
            out_ref[:B, :B] = product

        @pl.when((col_index < PANEL_BLOCKS) & (row_index == col_index))
        def _():
            out_ref[:B, :B] = u_own[...].T


def tile(xr, xc, m, y, u, damp):
    rows_here, cols_here = ROW_BLOCKS * B, COL_BLOCKS * B
    steps = ROW_BLOCKS // STEP_BLOCKS
    held = [*xc, *y, *u, m]
    return pl.pallas_call(
        functools.partial(tile_kernel, len(xr), len(xc)),
        grid=(steps + 1,),
        in_specs=[
            pl.BlockSpec((STEP_BLOCKS,) + piece.shape[1:], lambda i: (jnp.minimum(i, steps - 1), 0, 0)) for piece in xr
        ]
        + [pl.BlockSpec(memory_space=pl.ANY)] * len(held)
        + [pl.BlockSpec(damp.shape, lambda i: (0, 0))],
        out_specs=pl.BlockSpec((STEP_BLOCKS * B, cols_here), lambda i: (jnp.maximum(i - 1, 0), 0)),
        scratch_shapes=[pltpu.VMEM((NEX, cols_here), jnp.bfloat16)] * 2
        + [
            pltpu.VMEM((len(xc),) + xc[0].shape, jnp.float32),
            pltpu.VMEM((NEX, NEX), jnp.float32),
            pltpu.VMEM((NEX, B), jnp.float32),
            pltpu.VMEM((B, B), jnp.float32),
            pltpu.SemaphoreType.DMA((3 + len(xc),)),
        ]
        + [pltpu.VMEM((STEP_BLOCKS * B, NEX), jnp.bfloat16)] * 4,
        out_shape=jax.ShapeDtypeStruct((rows_here, cols_here), jnp.float32),
        compiler_params=pltpu.CompilerParams(vmem_limit_bytes=TILE_VMEM),
        cost_estimate=pl.CostEstimate(flops=12_000_000_000, bytes_accessed=24_000_000, transcendentals=0),
        name="tile",
    )(*xr, *held, damp)


def moved(value, target):
    pairs = [(row * N_COL + col, target(row, col)) for row in range(N_ROW) for col in range(N_COL)]
    return lax.ppermute(value, ("row", "col"), pairs)


def swapped(value, mask):
    return moved(value, lambda row, col: row * N_COL + (col ^ mask))


def swapped_rows(value, mask):
    return moved(value, lambda row, col: (row ^ mask) * N_COL + col)


FAR, RING, CORE = 8, (2, 4, 6), 1
NEXT, LINE = 4, (1, 2, 3)


def shards(activations, out_grads, proj_act, proj_grad, damping):
    row_index = lax.axis_index("row")
    col_index = lax.axis_index("col")
    act_sketch = jnp.dot(activations, proj_act, preferred_element_type=jnp.float32)
    grad_sketch = jnp.dot(out_grads, proj_grad, preferred_element_type=jnp.float32)
    here = activations.shape[0] // TOK_EX
    sketches = jnp.einsum(
        "eti,etj->eij",
        act_sketch.reshape(here, TOK_EX, SA),
        grad_sketch.reshape(here, TOK_EX, SG),
        precision=PRECISE,
    ) * (TOK_EX * NEX) ** (-0.5)

    for_rows = sketches.reshape(here, ROW_BLOCKS, N_ROW, B).transpose(2, 1, 0, 3)
    for_panel = jnp.broadcast_to(
        sketches[:, :PANEL_BLOCKS].transpose(1, 0, 2), (N_ROW, PANEL_BLOCKS, here, B)
    )
    parcels = lax.all_to_all(jnp.concatenate([for_rows, for_panel], 1), "row", split_axis=0, concat_axis=0)
    group = N_ROW * here
    parcels = parcels.transpose(1, 0, 2, 3).reshape(ROW_BLOCKS + PANEL_BLOCKS, group, B)
    rows = parcels[:ROW_BLOCKS]
    panel = parcels[ROW_BLOCKS:]

    parity = col_index % 2
    split = rows.reshape(COL_BLOCKS, 2, group, B)
    near = lax.dynamic_index_in_dim(split, parity, 1, keepdims=False)
    other = lax.dynamic_index_in_dim(split, 1 - parity, 1, keepdims=False)
    tie = lax.optimization_barrier
    panel = jnp.concatenate([panel, swapped(panel, FAR)], 1)
    panels = [panel] + [swapped(panel, mask) for mask in RING]
    near = jnp.concatenate([near, swapped(other, CORE)], 1)
    panels, near, rows = tie((panels, near, rows))
    panels = panels + [swapped(piece, CORE) for piece in panels]
    cols = [
        moved(near, lambda row, col: (col // 2 ^ mask) * N_COL + row + N_ROW * (col % 2)) for mask in (0, NEXT)
    ]
    rows_far = swapped(rows, FAR)

    damp_blocks = damping.reshape(SA, B)
    m, y0, u0, square = chain(panels, damp_blocks, 0, None)
    m, cols, rows, rows_far = tie((m, cols, rows, rows_far))
    rows = jnp.concatenate([rows, rows_far], 1)
    pieces = [rows] + [swapped(rows, mask) for mask in RING]
    cols = jnp.concatenate(cols, 1)
    xc = [cols] + [swapped_rows(cols, mask) for mask in LINE]
    m, y1, u1, square = chain(panels, damp_blocks, 1, [m, square, y0])
    m, y2, u2, square = chain(panels, damp_blocks, 2, [m, square, y1])
    m, pieces = tie((m, pieces))
    pieces = pieces + [swapped(piece, CORE) for piece in pieces]
    m, y3, u3, square = chain(panels, damp_blocks, 3, [m, square, y2])
    return tile(pieces, xc, m, (y0, y1, y2, y3), (u0, u1, u2, u3), damp_blocks)


def solution(mesh):
    placed = (P(("row", "col"), None), P(("row", "col"), None), P(), P(), P())
    return jax.shard_map(
        shards, mesh=mesh, in_specs=placed, out_specs=P("row", "col"), check_vma=False
    )
```

```python
import functools

import jax
import jax.numpy as jnp
from jax import lax
from jax.experimental import pallas as pl
from jax.experimental.pallas import tpu as pltpu
from jax.sharding import PartitionSpec as P

SA = 160
SG = 128
TOK_EX = 64
B = 128
PW = 512
PANELS = 2
NEX = 512
F = SA * SG
N_ROW = 8
N_COL = 16
FINISHED = PW * PANELS
PANEL_BLOCKS = FINISHED // B
CALLS = (2, 2, 2, 2)
FIRSTS = (0, 2, 4, 6)
STEP_BLOCKS = 4
CHAIN_VMEM = 24 << 20
TILE_VMEM = 32 << 20
ROW_BLOCKS = SA // N_ROW
COL_BLOCKS = SA // N_COL

PRECISE = lax.Precision.HIGHEST


def contract(left, right, left_dim, right_dim):
    return lax.dot_general(
        left,
        right,
        (((left_dim,), (right_dim,)), ((), ())),
        precision=PRECISE,
        preferred_element_type=jnp.float32,
    )


def single(left, right):
    return jnp.dot(left, right, preferred_element_type=jnp.float32)


def halves(value):
    high = value.astype(jnp.bfloat16)
    return high, (value - high.astype(jnp.float32)).astype(jnp.bfloat16)


def eliminate(square):
    sub = lax.broadcasted_iota(jnp.int32, (8, B), 0)
    lane = lax.broadcasted_iota(jnp.int32, (8, B), 1)
    tiles = [square[8 * t : 8 * t + 8, :] for t in range(B // 8)]
    for group in range(B // 8):
        first = 8 * group
        cols = {}
        for t in range(group, B // 8):
            for w in range(8):
                cols[t, w] = jnp.broadcast_to(tiles[t][:, first + w : first + w + 1], (8, B))
        scale = None
        for w in range(8):
            here = lane == first + w
            pivot = jnp.broadcast_to(cols[group, w][w : w + 1, :], (8, B))
            later = [jnp.broadcast_to(cols[group, v][w : w + 1, :], (8, B)) for v in range(w + 1, 8)]
            inverse = 1.0 / pivot
            row = jnp.where(here, 1.0, jnp.broadcast_to(tiles[group][w : w + 1, :], (8, B)))
            for t in range(group, B // 8):
                column = cols[t, w]
                cleared = here
                if t == group:
                    column = jnp.where(sub > w, column, 0.0)
                    cleared = here & (sub > w)
                ratio = column * inverse
                for v in range(w + 1, 8):
                    cols[t, v] = cols[t, v] - ratio * later[v - w - 1]
                tiles[t] = jnp.where(cleared, 0.0, tiles[t]) - ratio * row
            root = lax.rsqrt(pivot)
            scale = root if scale is None else jnp.where(sub >= w, root, scale)
        tiles[group] = jnp.where(lane == sub + first, scale, tiles[group] * scale)
    lower = [jnp.where(lane <= sub + 8 * t, tile, 0.0) for t, tile in enumerate(tiles)]
    upper = [
        jnp.where(lane > sub + 8 * t, tile, jnp.where(lane == sub + 8 * t, 1.0 / tile, 0.0))
        for t, tile in enumerate(tiles)
    ]
    return jnp.concatenate(upper, 0), jnp.concatenate(lower, 0)


def chain_kernel(call, pieces, *refs):
    first = call == 0
    final = call == len(CALLS) - 1
    count = CALLS[call]
    x_refs, refs = refs[:pieces], refs[pieces:]
    after_refs = ()
    if not final:
        after_refs, refs = refs[:pieces], refs[pieces:]
    if first:
        damp_ref, m_ref, y_ref, u_ref, s_ref, x_ref, last_ref = refs
    else:
        damp_ref, start_ref, square_ref, before_ref, m_ref, y_ref, u_ref, s_ref, x_ref, last_ref = refs
    ahead_last = count - 1 if final else count
    first_block = FIRSTS[call]
    down = lax.broadcasted_iota(jnp.int32, (B, B), 0)
    along = lax.broadcasted_iota(jnp.int32, (B, B), 1)

    def ridge(k):
        return jnp.where(down == along, jnp.broadcast_to(damp_ref[pl.ds(k, 1), :], (B, B)), 0.0)

    for k in range(count):
        x_ref[k] = jnp.concatenate([ref[k] for ref in x_refs], 0)
    if not final:
        x_ref[count] = jnp.concatenate([ref[0] for ref in after_refs], 0)
    if first:
        one = lax.broadcasted_iota(jnp.int32, (NEX, NEX), 0) == lax.broadcasted_iota(jnp.int32, (NEX, NEX), 1)
        m_ref[...] = jnp.where(one, 1.0, 0.0)
        block = x_ref[0]
        s_ref[...] = contract(block.T, block, 1, 0) + ridge(0)
        last_ref[...] = jnp.zeros_like(last_ref)
    else:
        m_ref[...] = start_ref[...]
        s_ref[...] = square_ref[...]
        last_ref[...] = before_ref[0]

    def body(k, carry):
        there = jnp.minimum(k + 1, ahead_last)
        square = s_ref[...]
        last = last_ref[...]
        m_now = m_ref[...] - contract(last, last, 1, 1)
        m_ref[...] = m_now
        following = x_ref[there]
        both = contract(m_now, jnp.concatenate([x_ref[k], following], 1), 1, 0)
        ahead = contract(following.T, both, 1, 0)
        upper, inverse = eliminate(square)
        below = contract(ahead[:, :B], inverse, 1, 1)
        s_ref[...] = ahead[:, B:] - contract(below, below, 1, 1) + ridge(first_block + there)
        y_now = contract(both[:, :B], inverse, 1, 1)
        last_ref[...] = y_now
        y_ref[k] = y_now
        u_ref[k] = upper
        return carry

    lax.fori_loop(0, count, body, 0)
    if final:
        last = last_ref[...]
        m_ref[...] = m_ref[...] - contract(last, last, 1, 1)


def chain(x, damp, call, state):
    first = call == 0
    final = call == len(CALLS) - 1
    count = CALLS[call]
    operands = list(x)
    specs = [pl.BlockSpec((count,) + piece.shape[1:], lambda i: (FIRSTS[call] // count, 0, 0)) for piece in x]
    if not final:
        operands += x
        specs += [pl.BlockSpec((1,) + piece.shape[1:], lambda i: (FIRSTS[call + 1], 0, 0)) for piece in x]
    operands.append(damp)
    specs.append(pl.BlockSpec(damp.shape, lambda i: (0, 0)))
    if not first:
        operands += state
        specs += [
            pl.BlockSpec((NEX, NEX), lambda i: (0, 0)),
            pl.BlockSpec((B, B), lambda i: (0, 0)),
            pl.BlockSpec((1, NEX, B), lambda i: (CALLS[call - 1] - 1, 0, 0)),
        ]
    shapes = ((NEX, NEX), (count, NEX, B), (count, B, B), (B, B))
    return pl.pallas_call(
        functools.partial(chain_kernel, call, len(x)),
        grid=(1,),
        in_specs=specs,
        out_specs=tuple(pl.BlockSpec(shape, lambda i, rank=len(shape): (0,) * rank) for shape in shapes),
        out_shape=tuple(jax.ShapeDtypeStruct(shape, jnp.float32) for shape in shapes),
        scratch_shapes=[
            pltpu.VMEM((count + 1, NEX, B), jnp.float32),
            pltpu.VMEM((NEX, B), jnp.float32),
        ],
        compiler_params=pltpu.CompilerParams(vmem_limit_bytes=CHAIN_VMEM),
        cost_estimate=pl.CostEstimate(
            flops=6_000_000_000 * count, bytes_accessed=16_000_000 * count, transcendentals=0
        ),
        name="chain",
    )(*operands)


def example_ids(row_index, col_index):
    at = lax.broadcasted_iota(jnp.int32, (NEX, 1), 0)
    mask = (at >> 8 & 1) * CORE + (at >> 6 & 3) * RING[0] + (at >> 5 & 1) * FAR
    row_ids = ((at >> 2 & 7) * N_COL + (col_index ^ mask)) * 4 + (at & 3)
    at = lax.broadcasted_iota(jnp.int32, (1, NEX), 1)
    source = row_index ^ (col_index & (N_ROW - 1)) ^ (at >> 7 & 3) ^ (at >> 6 & 1) * NEXT
    half = jnp.where(col_index >= N_ROW, 1, 0) ^ (at >> 5 & 1)
    col_ids = ((at >> 2 & 7) * N_COL + 2 * source + half) * 4 + (at & 3)
    return row_ids, col_ids


def tile_kernel(row_pieces, col_pieces, *refs):
    xr_refs, refs = refs[:row_pieces], refs[row_pieces:]
    xc_refs, refs = refs[:col_pieces], refs[col_pieces:]
    calls = len(CALLS)
    y_refs, refs = refs[:calls], refs[calls:]
    u_refs, refs = refs[:calls], refs[calls:]
    m_ref, damp_ref, out_ref, high_ref, low_ref, xc_own, m_own, y_own, u_own, sems = refs[:10]
    lefts = (refs[10:12], refs[12:14])
    step = pl.program_id(0)
    row_index = lax.axis_index("row")
    col_index = lax.axis_index("col")
    cols_here = out_ref.shape[1]
    chosen = [(col_index >= first) & (col_index < first + count) for first, count in zip(FIRSTS, CALLS)]
    in_call = [jnp.clip(col_index - first, 0, count - 1) for first, count in zip(FIRSTS, CALLS)]

    def m_copy():
        return pltpu.make_async_copy(m_ref, m_own, sems.at[0])

    def xc_copy(piece):
        return pltpu.make_async_copy(xc_refs[piece], xc_own.at[piece], sems.at[3 + piece])

    def y_copy(call):
        return pltpu.make_async_copy(y_refs[call].at[in_call[call]], y_own, sems.at[1])

    def u_copy(call):
        return pltpu.make_async_copy(u_refs[call].at[in_call[call]], u_own, sems.at[2])

    def turn(slot):
        for k in range(STEP_BLOCKS):
            left = jnp.concatenate([ref[k] for ref in xr_refs], 0).T
            for ref, part in zip(lefts[slot], halves(left)):
                ref[k * B : (k + 1) * B, :] = part

    def multiply(slot):
        for top in range(0, STEP_BLOCKS * B, 256):
            left_high = lefts[slot][0][top : top + 256, :]
            left_low = lefts[slot][1][top : top + 256, :]
            for start in range(0, cols_here, 256):
                high = high_ref[:, start : start + 256]
                low = low_ref[:, start : start + 256]
                out_ref[top : top + 256, start : start + 256] = (
                    single(left_high, high) + single(left_high, low) + single(left_low, high)
                )

    @pl.when(step == 0)
    def _():
        m_copy().start()
        for piece in range(col_pieces):
            xc_copy(piece).start()
        for call in range(calls):

            @pl.when(chosen[call])
            def _(call=call):
                y_copy(call).start()

            @pl.when(chosen[call] & (row_index == col_index))
            def _(call=call):
                u_copy(call).start()

        row_ids, col_ids = example_ids(row_index, col_index)
        to_cols = jnp.where(row_ids == col_ids, 1.0, 0.0).astype(jnp.bfloat16)
        turn(0)
        m_copy().wait()
        m_high, m_low = [single(part, to_cols).astype(jnp.bfloat16) for part in halves(m_own[...])]
        for piece in range(col_pieces):
            xc_copy(piece).wait()
        for start in range(0, COL_BLOCKS, 2):
            columns = [jnp.concatenate([xc_own[piece, start + k] for piece in range(col_pieces)], 0) for k in range(2)]
            x_high, x_low = halves(jnp.concatenate(columns, 1))
            right = single(m_high, x_high) + single(m_high, x_low) + single(m_low, x_high)
            high, low = halves(right)
            high_ref[:, start * B : (start + 2) * B] = high
            low_ref[:, start * B : (start + 2) * B] = low

        for call in range(calls):

            @pl.when(chosen[call])
            def _(call=call):
                y_copy(call).wait()
                high, low = halves(y_own[...])
                high_ref[:, :B] = high
                low_ref[:, :B] = low

            @pl.when(chosen[call] & (row_index == col_index))
            def _(call=call):
                u_copy(call).wait()

    for slot in range(2):

        @pl.when((step > 0) & ((step + 1) % 2 == slot))
        def _(slot=slot):
            multiply(slot)
            turn(1 - slot)

    @pl.when((step > 0) & (row_index == col_index % N_ROW))
    def _():
        down = lax.broadcasted_iota(jnp.int32, (B, B), 0)
        along = lax.broadcasted_iota(jnp.int32, (B, B), 1)
        upper_half = col_index // N_ROW
        for k in range(STEP_BLOCKS // 2):
            block = (step - 1) * (STEP_BLOCKS // 2) + k
            rows = pl.ds(pl.multiple_of((2 * k + upper_half) * B, B), B)
            cols = pl.ds(pl.multiple_of(block * B, B), B)
            ridge = jnp.broadcast_to(damp_ref[pl.ds(col_index + N_COL * block, 1), :], (B, B))
            out_ref[rows, cols] = out_ref[rows, cols] + jnp.where(down == along, ridge, 0.0)

    @pl.when(step == 1)
    def _():
        product = out_ref[:B, :B]
        out_ref[:B, :] = jnp.zeros((B, cols_here), jnp.float32)

        @pl.when((col_index < PANEL_BLOCKS) & (row_index > col_index))
        def _():
            out_ref[:B, :B] = product

        @pl.when((col_index < PANEL_BLOCKS) & (row_index == col_index))
        def _():
            out_ref[:B, :B] = u_own[...].T


def tile(xr, xc, m, y, u, damp):
    rows_here, cols_here = ROW_BLOCKS * B, COL_BLOCKS * B
    steps = ROW_BLOCKS // STEP_BLOCKS
    held = [*xc, *y, *u, m]
    return pl.pallas_call(
        functools.partial(tile_kernel, len(xr), len(xc)),
        grid=(steps + 1,),
        in_specs=[
            pl.BlockSpec((STEP_BLOCKS,) + piece.shape[1:], lambda i: (jnp.minimum(i, steps - 1), 0, 0)) for piece in xr
        ]
        + [pl.BlockSpec(memory_space=pl.ANY)] * len(held)
        + [pl.BlockSpec(damp.shape, lambda i: (0, 0))],
        out_specs=pl.BlockSpec((STEP_BLOCKS * B, cols_here), lambda i: (jnp.maximum(i - 1, 0), 0)),
        scratch_shapes=[pltpu.VMEM((NEX, cols_here), jnp.bfloat16)] * 2
        + [
            pltpu.VMEM((len(xc),) + xc[0].shape, jnp.float32),
            pltpu.VMEM((NEX, NEX), jnp.float32),
            pltpu.VMEM((NEX, B), jnp.float32),
            pltpu.VMEM((B, B), jnp.float32),
            pltpu.SemaphoreType.DMA((3 + len(xc),)),
        ]
        + [pltpu.VMEM((STEP_BLOCKS * B, NEX), jnp.bfloat16)] * 4,
        out_shape=jax.ShapeDtypeStruct((rows_here, cols_here), jnp.float32),
        compiler_params=pltpu.CompilerParams(vmem_limit_bytes=TILE_VMEM),
        cost_estimate=pl.CostEstimate(flops=12_000_000_000, bytes_accessed=24_000_000, transcendentals=0),
        name="tile",
    )(*xr, *held, damp)


def moved(value, target):
    pairs = [(row * N_COL + col, target(row, col)) for row in range(N_ROW) for col in range(N_COL)]
    return lax.ppermute(value, ("row", "col"), pairs)


def swapped(value, mask):
    return moved(value, lambda row, col: row * N_COL + (col ^ mask))


def swapped_rows(value, mask):
    return moved(value, lambda row, col: (row ^ mask) * N_COL + col)


FAR, RING, CORE = 8, (2, 4, 6), 1
NEXT, LINE = 4, (1, 2, 3)


def shards(activations, out_grads, proj_act, proj_grad, damping):
    row_index = lax.axis_index("row")
    col_index = lax.axis_index("col")
    act_sketch = jnp.dot(activations, proj_act, preferred_element_type=jnp.float32)
    grad_sketch = jnp.dot(out_grads, proj_grad, preferred_element_type=jnp.float32)
    here = activations.shape[0] // TOK_EX
    sketches = jnp.einsum(
        "eti,etj->eij",
        act_sketch.reshape(here, TOK_EX, SA),
        grad_sketch.reshape(here, TOK_EX, SG),
        precision=PRECISE,
    ) * (TOK_EX * NEX) ** (-0.5)

    for_rows = sketches.reshape(here, ROW_BLOCKS, N_ROW, B).transpose(2, 1, 0, 3)
    for_panel = jnp.broadcast_to(
        sketches[:, :PANEL_BLOCKS].transpose(1, 0, 2), (N_ROW, PANEL_BLOCKS, here, B)
    )
    parcels = lax.all_to_all(jnp.concatenate([for_rows, for_panel], 1), "row", split_axis=0, concat_axis=0)
    group = N_ROW * here
    parcels = parcels.transpose(1, 0, 2, 3).reshape(ROW_BLOCKS + PANEL_BLOCKS, group, B)
    rows = parcels[:ROW_BLOCKS]
    panel = parcels[ROW_BLOCKS:]

    parity = col_index % 2
    split = rows.reshape(COL_BLOCKS, 2, group, B)
    near = lax.dynamic_index_in_dim(split, parity, 1, keepdims=False)
    other = lax.dynamic_index_in_dim(split, 1 - parity, 1, keepdims=False)
    tie = lax.optimization_barrier
    panel = jnp.concatenate([panel, swapped(panel, FAR)], 1)
    panels = [panel] + [swapped(panel, mask) for mask in RING]
    near = jnp.concatenate([near, swapped(other, CORE)], 1)
    panels, near, rows = tie((panels, near, rows))
    panels = panels + [swapped(piece, CORE) for piece in panels]
    cols = [
        moved(near, lambda row, col: (col // 2 ^ row ^ mask) * N_COL + row + N_ROW * (col % 2)) for mask in (0, NEXT)
    ]
    rows_far = swapped(rows, FAR)

    damp_blocks = damping.reshape(SA, B)
    m, y0, u0, square = chain(panels, damp_blocks, 0, None)
    m, cols, rows, rows_far = tie((m, cols, rows, rows_far))
    rows = jnp.concatenate([rows, rows_far], 1)
    pieces = [rows] + [swapped(rows, mask) for mask in RING]
    cols = jnp.concatenate(cols, 1)
    xc = [cols] + [swapped_rows(cols, mask) for mask in LINE]
    m, y1, u1, square = chain(panels, damp_blocks, 1, [m, square, y0])
    m, y2, u2, square = chain(panels, damp_blocks, 2, [m, square, y1])
    m, pieces = tie((m, pieces))
    pieces = pieces + [swapped(piece, CORE) for piece in pieces]
    m, y3, u3, square = chain(panels, damp_blocks, 3, [m, square, y2])
    return tile(pieces, xc, m, (y0, y1, y2, y3), (u0, u1, u2, u3), damp_blocks)


def solution(mesh):
    placed = (P(("row", "col"), None), P(("row", "col"), None), P(), P(), P())
    return jax.shard_map(
        shards, mesh=mesh, in_specs=placed, out_specs=P("row", "col"), check_vma=False
    )
```

```python
import functools

import jax
import jax.numpy as jnp
from jax import lax
from jax.experimental import pallas as pl
from jax.experimental.pallas import tpu as pltpu
from jax.sharding import PartitionSpec as P

SA = 160
SG = 128
TOK_EX = 64
B = 128
PW = 512
PANELS = 2
NEX = 512
F = SA * SG
N_ROW = 8
N_COL = 16
FINISHED = PW * PANELS
PANEL_BLOCKS = FINISHED // B
CALLS = (2, 2, 2, 2)
FIRSTS = (0, 2, 4, 6)
STEP_BLOCKS = 4
CHAIN_VMEM = 24 << 20
TILE_VMEM = 32 << 20
ROW_BLOCKS = SA // N_ROW
COL_BLOCKS = SA // N_COL

PRECISE = lax.Precision.HIGHEST


def contract(left, right, left_dim, right_dim):
    return lax.dot_general(
        left,
        right,
        (((left_dim,), (right_dim,)), ((), ())),
        precision=PRECISE,
        preferred_element_type=jnp.float32,
    )


def single(left, right):
    return jnp.dot(left, right, preferred_element_type=jnp.float32)


def halves(value):
    high = value.astype(jnp.bfloat16)
    return high, (value - high.astype(jnp.float32)).astype(jnp.bfloat16)


def eliminate(square):
    sub = lax.broadcasted_iota(jnp.int32, (8, B), 0)
    lane = lax.broadcasted_iota(jnp.int32, (8, B), 1)
    tiles = [square[8 * t : 8 * t + 8, :] for t in range(B // 8)]
    for group in range(B // 8):
        first = 8 * group
        cols = {}
        for t in range(group, B // 8):
            for w in range(8):
                cols[t, w] = jnp.broadcast_to(tiles[t][:, first + w : first + w + 1], (8, B))
        scale = None
        for w in range(8):
            here = lane == first + w
            pivot = jnp.broadcast_to(cols[group, w][w : w + 1, :], (8, B))
            later = [jnp.broadcast_to(cols[group, v][w : w + 1, :], (8, B)) for v in range(w + 1, 8)]
            inverse = 1.0 / pivot
            row = jnp.where(here, 1.0, jnp.broadcast_to(tiles[group][w : w + 1, :], (8, B)))
            for t in range(group, B // 8):
                column = cols[t, w]
                cleared = here
                if t == group:
                    column = jnp.where(sub > w, column, 0.0)
                    cleared = here & (sub > w)
                ratio = column * inverse
                for v in range(w + 1, 8):
                    cols[t, v] = cols[t, v] - ratio * later[v - w - 1]
                tiles[t] = jnp.where(cleared, 0.0, tiles[t]) - ratio * row
            root = lax.rsqrt(pivot)
            scale = root if scale is None else jnp.where(sub >= w, root, scale)
        tiles[group] = jnp.where(lane == sub + first, scale, tiles[group] * scale)
    lower = [jnp.where(lane <= sub + 8 * t, tile, 0.0) for t, tile in enumerate(tiles)]
    upper = [
        jnp.where(lane > sub + 8 * t, tile, jnp.where(lane == sub + 8 * t, 1.0 / tile, 0.0))
        for t, tile in enumerate(tiles)
    ]
    return jnp.concatenate(upper, 0), jnp.concatenate(lower, 0)


def chain_kernel(call, pieces, *refs):
    first = call == 0
    final = call == len(CALLS) - 1
    count = CALLS[call]
    x_refs, refs = refs[:pieces], refs[pieces:]
    after_refs = ()
    if not final:
        after_refs, refs = refs[:pieces], refs[pieces:]
    if first:
        damp_ref, m_ref, y_ref, u_ref, s_ref, x_ref, last_ref = refs
    else:
        damp_ref, start_ref, square_ref, before_ref, m_ref, y_ref, u_ref, s_ref, x_ref, last_ref = refs
    ahead_last = count - 1 if final else count
    first_block = FIRSTS[call]
    down = lax.broadcasted_iota(jnp.int32, (B, B), 0)
    along = lax.broadcasted_iota(jnp.int32, (B, B), 1)

    def ridge(k):
        return jnp.where(down == along, jnp.broadcast_to(damp_ref[pl.ds(k, 1), :], (B, B)), 0.0)

    for k in range(count):
        x_ref[k] = jnp.concatenate([ref[k] for ref in x_refs], 0)
    if not final:
        x_ref[count] = jnp.concatenate([ref[0] for ref in after_refs], 0)
    if first:
        one = lax.broadcasted_iota(jnp.int32, (NEX, NEX), 0) == lax.broadcasted_iota(jnp.int32, (NEX, NEX), 1)
        m_ref[...] = jnp.where(one, 1.0, 0.0)
        block = x_ref[0]
        s_ref[...] = contract(block.T, block, 1, 0) + ridge(0)
        last_ref[...] = jnp.zeros_like(last_ref)
    else:
        m_ref[...] = start_ref[...]
        s_ref[...] = square_ref[...]
        last_ref[...] = before_ref[0]

    def body(k, carry):
        there = jnp.minimum(k + 1, ahead_last)
        square = s_ref[...]
        last = last_ref[...]
        m_now = m_ref[...] - contract(last, last, 1, 1)
        m_ref[...] = m_now
        following = x_ref[there]
        both = contract(m_now, jnp.concatenate([x_ref[k], following], 1), 1, 0)
        ahead = contract(following.T, both, 1, 0)
        upper, inverse = eliminate(square)
        below = contract(ahead[:, :B], inverse, 1, 1)
        s_ref[...] = ahead[:, B:] - contract(below, below, 1, 1) + ridge(first_block + there)
        y_now = contract(both[:, :B], inverse, 1, 1)
        last_ref[...] = y_now
        y_ref[k] = y_now
        u_ref[k] = upper
        return carry

    lax.fori_loop(0, count, body, 0)
    if final:
        last = last_ref[...]
        m_ref[...] = m_ref[...] - contract(last, last, 1, 1)


def chain(x, damp, call, state):
    first = call == 0
    final = call == len(CALLS) - 1
    count = CALLS[call]
    operands = list(x)
    specs = [pl.BlockSpec((count,) + piece.shape[1:], lambda i: (FIRSTS[call] // count, 0, 0)) for piece in x]
    if not final:
        operands += x
        specs += [pl.BlockSpec((1,) + piece.shape[1:], lambda i: (FIRSTS[call + 1], 0, 0)) for piece in x]
    operands.append(damp)
    specs.append(pl.BlockSpec(damp.shape, lambda i: (0, 0)))
    if not first:
        operands += state
        specs += [
            pl.BlockSpec((NEX, NEX), lambda i: (0, 0)),
            pl.BlockSpec((B, B), lambda i: (0, 0)),
            pl.BlockSpec((1, NEX, B), lambda i: (CALLS[call - 1] - 1, 0, 0)),
        ]
    shapes = ((NEX, NEX), (count, NEX, B), (count, B, B), (B, B))
    return pl.pallas_call(
        functools.partial(chain_kernel, call, len(x)),
        grid=(1,),
        in_specs=specs,
        out_specs=tuple(pl.BlockSpec(shape, lambda i, rank=len(shape): (0,) * rank) for shape in shapes),
        out_shape=tuple(jax.ShapeDtypeStruct(shape, jnp.float32) for shape in shapes),
        scratch_shapes=[
            pltpu.VMEM((count + 1, NEX, B), jnp.float32),
            pltpu.VMEM((NEX, B), jnp.float32),
        ],
        compiler_params=pltpu.CompilerParams(vmem_limit_bytes=CHAIN_VMEM),
        cost_estimate=pl.CostEstimate(
            flops=600_000_000 * count, bytes_accessed=2_000_000 * count, transcendentals=0
        ),
        name="chain",
    )(*operands)


def example_ids(row_index, col_index):
    at = lax.broadcasted_iota(jnp.int32, (NEX, 1), 0)
    mask = (at >> 8 & 1) * CORE + (at >> 6 & 3) * RING[0] + (at >> 5 & 1) * FAR
    row_ids = ((at >> 2 & 7) * N_COL + (col_index ^ mask)) * 4 + (at & 3)
    at = lax.broadcasted_iota(jnp.int32, (1, NEX), 1)
    source = row_index ^ (col_index & (N_ROW - 1)) ^ (at >> 7 & 3) ^ (at >> 6 & 1) * NEXT
    half = jnp.where(col_index >= N_ROW, 1, 0) ^ (at >> 5 & 1)
    col_ids = ((at >> 2 & 7) * N_COL + 2 * source + half) * 4 + (at & 3)
    return row_ids, col_ids


def tile_kernel(row_pieces, col_pieces, *refs):
    xr_refs, refs = refs[:row_pieces], refs[row_pieces:]
    xc_refs, refs = refs[:col_pieces], refs[col_pieces:]
    calls = len(CALLS)
    y_refs, refs = refs[:calls], refs[calls:]
    u_refs, refs = refs[:calls], refs[calls:]
    m_ref, damp_ref, out_ref, high_ref, low_ref, xc_own, m_own, y_own, u_own, sems = refs[:10]
    lefts = (refs[10:12], refs[12:14])
    step = pl.program_id(0)
    row_index = lax.axis_index("row")
    col_index = lax.axis_index("col")
    cols_here = out_ref.shape[1]
    chosen = [(col_index >= first) & (col_index < first + count) for first, count in zip(FIRSTS, CALLS)]
    in_call = [jnp.clip(col_index - first, 0, count - 1) for first, count in zip(FIRSTS, CALLS)]

    def m_copy():
        return pltpu.make_async_copy(m_ref, m_own, sems.at[0])

    def xc_copy(piece):
        return pltpu.make_async_copy(xc_refs[piece], xc_own.at[piece], sems.at[3 + piece])

    def y_copy(call):
        return pltpu.make_async_copy(y_refs[call].at[in_call[call]], y_own, sems.at[1])

    def u_copy(call):
        return pltpu.make_async_copy(u_refs[call].at[in_call[call]], u_own, sems.at[2])

    def turn(slot):
        for k in range(STEP_BLOCKS):
            left = jnp.concatenate([ref[k] for ref in xr_refs], 0).T
            for ref, part in zip(lefts[slot], halves(left)):
                ref[k * B : (k + 1) * B, :] = part

    def multiply(slot):
        for top in range(0, STEP_BLOCKS * B, 256):
            left_high = lefts[slot][0][top : top + 256, :]
            left_low = lefts[slot][1][top : top + 256, :]
            for start in range(0, cols_here, 256):
                high = high_ref[:, start : start + 256]
                low = low_ref[:, start : start + 256]
                out_ref[top : top + 256, start : start + 256] = (
                    single(left_high, high) + single(left_high, low) + single(left_low, high)
                )

    @pl.when(step == 0)
    def _():
        m_copy().start()
        for piece in range(col_pieces):
            xc_copy(piece).start()
        for call in range(calls):

            @pl.when(chosen[call])
            def _(call=call):
                y_copy(call).start()

            @pl.when(chosen[call] & (row_index == col_index))
            def _(call=call):
                u_copy(call).start()

        row_ids, col_ids = example_ids(row_index, col_index)
        to_cols = jnp.where(row_ids == col_ids, 1.0, 0.0).astype(jnp.bfloat16)
        turn(0)
        m_copy().wait()
        m_high, m_low = [single(part, to_cols).astype(jnp.bfloat16) for part in halves(m_own[...])]
        for piece in range(col_pieces):
            xc_copy(piece).wait()
        for start in range(0, COL_BLOCKS, 2):
            columns = [jnp.concatenate([xc_own[piece, start + k] for piece in range(col_pieces)], 0) for k in range(2)]
            x_high, x_low = halves(jnp.concatenate(columns, 1))
            right = single(m_high, x_high) + single(m_high, x_low) + single(m_low, x_high)
            high, low = halves(right)
            high_ref[:, start * B : (start + 2) * B] = high
            low_ref[:, start * B : (start + 2) * B] = low

        for call in range(calls):

            @pl.when(chosen[call])
            def _(call=call):
                y_copy(call).wait()
                high, low = halves(y_own[...])
                high_ref[:, :B] = high
                low_ref[:, :B] = low

            @pl.when(chosen[call] & (row_index == col_index))
            def _(call=call):
                u_copy(call).wait()

    for slot in range(2):

        @pl.when((step > 0) & ((step + 1) % 2 == slot))
        def _(slot=slot):
            multiply(slot)
            turn(1 - slot)

    @pl.when((step > 0) & (row_index == col_index % N_ROW))
    def _():
        down = lax.broadcasted_iota(jnp.int32, (B, B), 0)
        along = lax.broadcasted_iota(jnp.int32, (B, B), 1)
        upper_half = col_index // N_ROW
        for k in range(STEP_BLOCKS // 2):
            block = (step - 1) * (STEP_BLOCKS // 2) + k
            rows = pl.ds(pl.multiple_of((2 * k + upper_half) * B, B), B)
            cols = pl.ds(pl.multiple_of(block * B, B), B)
            ridge = jnp.broadcast_to(damp_ref[pl.ds(col_index + N_COL * block, 1), :], (B, B))
            out_ref[rows, cols] = out_ref[rows, cols] + jnp.where(down == along, ridge, 0.0)

    @pl.when(step == 1)
    def _():
        product = out_ref[:B, :B]
        out_ref[:B, :] = jnp.zeros((B, cols_here), jnp.float32)

        @pl.when((col_index < PANEL_BLOCKS) & (row_index > col_index))
        def _():
            out_ref[:B, :B] = product

        @pl.when((col_index < PANEL_BLOCKS) & (row_index == col_index))
        def _():
            out_ref[:B, :B] = u_own[...].T


def tile(xr, xc, m, y, u, damp):
    rows_here, cols_here = ROW_BLOCKS * B, COL_BLOCKS * B
    steps = ROW_BLOCKS // STEP_BLOCKS
    held = [*xc, *y, *u, m]
    return pl.pallas_call(
        functools.partial(tile_kernel, len(xr), len(xc)),
        grid=(steps + 1,),
        in_specs=[
            pl.BlockSpec((STEP_BLOCKS,) + piece.shape[1:], lambda i: (jnp.minimum(i, steps - 1), 0, 0)) for piece in xr
        ]
        + [pl.BlockSpec(memory_space=pl.ANY)] * len(held)
        + [pl.BlockSpec(damp.shape, lambda i: (0, 0))],
        out_specs=pl.BlockSpec((STEP_BLOCKS * B, cols_here), lambda i: (jnp.maximum(i - 1, 0), 0)),
        scratch_shapes=[pltpu.VMEM((NEX, cols_here), jnp.bfloat16)] * 2
        + [
            pltpu.VMEM((len(xc),) + xc[0].shape, jnp.float32),
            pltpu.VMEM((NEX, NEX), jnp.float32),
            pltpu.VMEM((NEX, B), jnp.float32),
            pltpu.VMEM((B, B), jnp.float32),
            pltpu.SemaphoreType.DMA((3 + len(xc),)),
        ]
        + [pltpu.VMEM((STEP_BLOCKS * B, NEX), jnp.bfloat16)] * 4,
        out_shape=jax.ShapeDtypeStruct((rows_here, cols_here), jnp.float32),
        compiler_params=pltpu.CompilerParams(vmem_limit_bytes=TILE_VMEM),
        cost_estimate=pl.CostEstimate(flops=12_000_000_000, bytes_accessed=24_000_000, transcendentals=0),
        name="tile",
    )(*xr, *held, damp)


def moved(value, target):
    pairs = [(row * N_COL + col, target(row, col)) for row in range(N_ROW) for col in range(N_COL)]
    return lax.ppermute(value, ("row", "col"), pairs)


def swapped(value, mask):
    return moved(value, lambda row, col: row * N_COL + (col ^ mask))


def swapped_rows(value, mask):
    return moved(value, lambda row, col: (row ^ mask) * N_COL + col)


FAR, RING, CORE = 8, (2, 4, 6), 1
NEXT, LINE = 4, (1, 2, 3)


def shards(activations, out_grads, proj_act, proj_grad, damping):
    row_index = lax.axis_index("row")
    col_index = lax.axis_index("col")
    act_sketch = jnp.dot(activations, proj_act, preferred_element_type=jnp.float32)
    grad_sketch = jnp.dot(out_grads, proj_grad, preferred_element_type=jnp.float32)
    here = activations.shape[0] // TOK_EX
    sketches = jnp.einsum(
        "eti,etj->eij",
        act_sketch.reshape(here, TOK_EX, SA),
        grad_sketch.reshape(here, TOK_EX, SG),
        precision=PRECISE,
    ) * (TOK_EX * NEX) ** (-0.5)

    for_rows = sketches.reshape(here, ROW_BLOCKS, N_ROW, B).transpose(2, 1, 0, 3)
    for_panel = jnp.broadcast_to(
        sketches[:, :PANEL_BLOCKS].transpose(1, 0, 2), (N_ROW, PANEL_BLOCKS, here, B)
    )
    parcels = lax.all_to_all(jnp.concatenate([for_rows, for_panel], 1), "row", split_axis=0, concat_axis=0)
    group = N_ROW * here
    parcels = parcels.transpose(1, 0, 2, 3).reshape(ROW_BLOCKS + PANEL_BLOCKS, group, B)
    rows = parcels[:ROW_BLOCKS]
    panel = parcels[ROW_BLOCKS:]

    parity = col_index % 2
    split = rows.reshape(COL_BLOCKS, 2, group, B)
    near = lax.dynamic_index_in_dim(split, parity, 1, keepdims=False)
    other = lax.dynamic_index_in_dim(split, 1 - parity, 1, keepdims=False)
    tie = lax.optimization_barrier
    panel = jnp.concatenate([panel, swapped(panel, FAR)], 1)
    panels = [panel] + [swapped(panel, mask) for mask in RING]
    near = jnp.concatenate([near, swapped(other, CORE)], 1)
    panels, near, rows = tie((panels, near, rows))
    panels = panels + [swapped(piece, CORE) for piece in panels]
    cols = [
        moved(near, lambda row, col: (col // 2 ^ row ^ mask) * N_COL + row + N_ROW * (col % 2)) for mask in (0, NEXT)
    ]
    rows_far = swapped(rows, FAR)

    damp_blocks = damping.reshape(SA, B)
    m, y0, u0, square = chain(panels, damp_blocks, 0, None)
    m, rows, rows_far = tie((m, rows, rows_far))
    rows = jnp.concatenate([rows, rows_far], 1)
    pieces = [rows] + [swapped(rows, mask) for mask in RING]
    m, y1, u1, square = chain(panels, damp_blocks, 1, [m, square, y0])
    m, cols = tie((m, cols))
    cols = jnp.concatenate(cols, 1)
    xc = [cols] + [swapped_rows(cols, mask) for mask in LINE]
    m, y2, u2, square = chain(panels, damp_blocks, 2, [m, square, y1])
    m, pieces = tie((m, pieces))
    pieces = pieces + [swapped(piece, CORE) for piece in pieces]
    m, y3, u3, square = chain(panels, damp_blocks, 3, [m, square, y2])
    return tile(pieces, xc, m, (y0, y1, y2, y3), (u0, u1, u2, u3), damp_blocks)


def solution(mesh):
    placed = (P(("row", "col"), None), P(("row", "col"), None), P(), P(), P())
    return jax.shard_map(
        shards, mesh=mesh, in_specs=placed, out_specs=P("row", "col"), check_vma=False
    )
```

```python
import functools

import jax
import jax.numpy as jnp
from jax import lax
from jax.experimental import pallas as pl
from jax.experimental.pallas import tpu as pltpu
from jax.sharding import PartitionSpec as P

SA = 160
SG = 128
TOK_EX = 64
B = 128
PW = 512
PANELS = 2
NEX = 512
F = SA * SG
N_ROW = 8
N_COL = 16
FINISHED = PW * PANELS
PANEL_BLOCKS = FINISHED // B
CALLS = (2, 4, 2)
FIRSTS = (0, 2, 6)
PAIR = 2
STEP_BLOCKS = 4
CHAIN_VMEM = 24 << 20
TILE_VMEM = 32 << 20
ROW_BLOCKS = SA // N_ROW
COL_BLOCKS = SA // N_COL

PRECISE = lax.Precision.HIGHEST


def contract(left, right, left_dim, right_dim):
    return lax.dot_general(
        left,
        right,
        (((left_dim,), (right_dim,)), ((), ())),
        precision=PRECISE,
        preferred_element_type=jnp.float32,
    )


def single(left, right):
    return jnp.dot(left, right, preferred_element_type=jnp.float32)


def halves(value):
    high = value.astype(jnp.bfloat16)
    return high, (value - high.astype(jnp.float32)).astype(jnp.bfloat16)


def eliminate(square):
    sub = lax.broadcasted_iota(jnp.int32, (8, B), 0)
    lane = lax.broadcasted_iota(jnp.int32, (8, B), 1)
    tiles = [square[8 * t : 8 * t + 8, :] for t in range(B // 8)]
    for group in range(B // 8):
        first = 8 * group
        cols = {}
        for t in range(group, B // 8):
            for w in range(8):
                cols[t, w] = jnp.broadcast_to(tiles[t][:, first + w : first + w + 1], (8, B))
        scale = None
        for w in range(8):
            here = lane == first + w
            pivot = jnp.broadcast_to(cols[group, w][w : w + 1, :], (8, B))
            later = [jnp.broadcast_to(cols[group, v][w : w + 1, :], (8, B)) for v in range(w + 1, 8)]
            inverse = 1.0 / pivot
            row = jnp.where(here, 1.0, jnp.broadcast_to(tiles[group][w : w + 1, :], (8, B)))
            for t in range(group, B // 8):
                column = cols[t, w]
                cleared = here
                if t == group:
                    column = jnp.where(sub > w, column, 0.0)
                    cleared = here & (sub > w)
                ratio = column * inverse
                for v in range(w + 1, 8):
                    cols[t, v] = cols[t, v] - ratio * later[v - w - 1]
                tiles[t] = jnp.where(cleared, 0.0, tiles[t]) - ratio * row
            root = lax.rsqrt(pivot)
            scale = root if scale is None else jnp.where(sub >= w, root, scale)
        tiles[group] = jnp.where(lane == sub + first, scale, tiles[group] * scale)
    lower = [jnp.where(lane <= sub + 8 * t, tile, 0.0) for t, tile in enumerate(tiles)]
    upper = [
        jnp.where(lane > sub + 8 * t, tile, jnp.where(lane == sub + 8 * t, 1.0 / tile, 0.0))
        for t, tile in enumerate(tiles)
    ]
    return jnp.concatenate(upper, 0), jnp.concatenate(lower, 0)


def chain_kernel(call, pieces, *refs):
    first = call == 0
    final = call == len(CALLS) - 1
    count = CALLS[call]
    pairs = []
    for _ in range(count // PAIR):
        pairs.append(refs[:pieces])
        refs = refs[pieces:]
    after_refs = ()
    if not final:
        after_refs, refs = refs[:pieces], refs[pieces:]
    if first:
        damp_ref, m_ref, y_ref, u_ref, s_ref, x_ref, last_ref = refs
    else:
        damp_ref, start_ref, square_ref, before_ref, m_ref, y_ref, u_ref, s_ref, x_ref, last_ref = refs
    ahead_last = count - 1 if final else count
    first_block = FIRSTS[call]
    down = lax.broadcasted_iota(jnp.int32, (B, B), 0)
    along = lax.broadcasted_iota(jnp.int32, (B, B), 1)

    def ridge(k):
        return jnp.where(down == along, jnp.broadcast_to(damp_ref[pl.ds(k, 1), :], (B, B)), 0.0)

    for k in range(count):
        x_ref[k] = jnp.concatenate([ref[k % PAIR] for ref in pairs[k // PAIR]], 0)
    if not final:
        x_ref[count] = jnp.concatenate([ref[0] for ref in after_refs], 0)
    if first:
        one = lax.broadcasted_iota(jnp.int32, (NEX, NEX), 0) == lax.broadcasted_iota(jnp.int32, (NEX, NEX), 1)
        m_ref[...] = jnp.where(one, 1.0, 0.0)
        block = x_ref[0]
        s_ref[...] = contract(block.T, block, 1, 0) + ridge(0)
        last_ref[...] = jnp.zeros_like(last_ref)
    else:
        m_ref[...] = start_ref[...]
        s_ref[...] = square_ref[...]
        last_ref[...] = before_ref[0]

    def body(k, carry):
        there = jnp.minimum(k + 1, ahead_last)
        square = s_ref[...]
        last = last_ref[...]
        m_now = m_ref[...] - contract(last, last, 1, 1)
        m_ref[...] = m_now
        following = x_ref[there]
        both = contract(m_now, jnp.concatenate([x_ref[k], following], 1), 1, 0)
        ahead = contract(following.T, both, 1, 0)
        upper, inverse = eliminate(square)
        below = contract(ahead[:, :B], inverse, 1, 1)
        s_ref[...] = ahead[:, B:] - contract(below, below, 1, 1) + ridge(first_block + there)
        y_now = contract(both[:, :B], inverse, 1, 1)
        last_ref[...] = y_now
        y_ref[k] = y_now
        u_ref[k] = upper
        return carry

    lax.fori_loop(0, count, body, 0)
    if final:
        last = last_ref[...]
        m_ref[...] = m_ref[...] - contract(last, last, 1, 1)


def chain(x, damp, call, state):
    first = call == 0
    final = call == len(CALLS) - 1
    count = CALLS[call]
    operands = []
    specs = []
    for pair in range(FIRSTS[call] // PAIR, (FIRSTS[call] + count) // PAIR):
        operands += x
        specs += [pl.BlockSpec((PAIR,) + piece.shape[1:], lambda i, pair=pair: (pair, 0, 0)) for piece in x]
    if not final:
        operands += x
        specs += [pl.BlockSpec((1,) + piece.shape[1:], lambda i: (FIRSTS[call + 1], 0, 0)) for piece in x]
    operands.append(damp)
    specs.append(pl.BlockSpec(damp.shape, lambda i: (0, 0)))
    if not first:
        operands += state
        specs += [
            pl.BlockSpec((NEX, NEX), lambda i: (0, 0)),
            pl.BlockSpec((B, B), lambda i: (0, 0)),
            pl.BlockSpec((1, NEX, B), lambda i: (CALLS[call - 1] - 1, 0, 0)),
        ]
    shapes = ((NEX, NEX), (count, NEX, B), (count, B, B), (B, B))
    return pl.pallas_call(
        functools.partial(chain_kernel, call, len(x)),
        grid=(1,),
        in_specs=specs,
        out_specs=tuple(pl.BlockSpec(shape, lambda i, rank=len(shape): (0,) * rank) for shape in shapes),
        out_shape=tuple(jax.ShapeDtypeStruct(shape, jnp.float32) for shape in shapes),
        scratch_shapes=[
            pltpu.VMEM((count + 1, NEX, B), jnp.float32),
            pltpu.VMEM((NEX, B), jnp.float32),
        ],
        compiler_params=pltpu.CompilerParams(vmem_limit_bytes=CHAIN_VMEM),
        cost_estimate=pl.CostEstimate(
            flops=600_000_000 * count, bytes_accessed=2_000_000 * count, transcendentals=0
        ),
        name="chain",
    )(*operands)


def example_ids(row_index, col_index):
    at = lax.broadcasted_iota(jnp.int32, (NEX, 1), 0)
    mask = (at >> 8 & 1) * CORE + (at >> 6 & 3) * RING[0] + (at >> 5 & 1) * FAR
    row_ids = ((at >> 2 & 7) * N_COL + (col_index ^ mask)) * 4 + (at & 3)
    at = lax.broadcasted_iota(jnp.int32, (1, NEX), 1)
    source = row_index ^ (col_index & (N_ROW - 1)) ^ (at >> 7 & 3) ^ (at >> 6 & 1) * NEXT
    half = jnp.where(col_index >= N_ROW, 1, 0) ^ (at >> 5 & 1)
    col_ids = ((at >> 2 & 7) * N_COL + 2 * source + half) * 4 + (at & 3)
    return row_ids, col_ids


def tile_kernel(row_pieces, col_pieces, *refs):
    xr_refs, refs = refs[:row_pieces], refs[row_pieces:]
    xc_refs, refs = refs[:col_pieces], refs[col_pieces:]
    calls = len(CALLS)
    y_refs, refs = refs[:calls], refs[calls:]
    u_refs, refs = refs[:calls], refs[calls:]
    m_ref, damp_ref, out_ref, high_ref, low_ref, xc_own, m_own, y_own, u_own, sems = refs[:10]
    lefts = (refs[10:12], refs[12:14])
    step = pl.program_id(0)
    row_index = lax.axis_index("row")
    col_index = lax.axis_index("col")
    cols_here = out_ref.shape[1]
    chosen = [(col_index >= first) & (col_index < first + count) for first, count in zip(FIRSTS, CALLS)]
    in_call = [jnp.clip(col_index - first, 0, count - 1) for first, count in zip(FIRSTS, CALLS)]

    def m_copy():
        return pltpu.make_async_copy(m_ref, m_own, sems.at[0])

    def xc_copy(piece):
        return pltpu.make_async_copy(xc_refs[piece], xc_own.at[piece], sems.at[3 + piece])

    def y_copy(call):
        return pltpu.make_async_copy(y_refs[call].at[in_call[call]], y_own, sems.at[1])

    def u_copy(call):
        return pltpu.make_async_copy(u_refs[call].at[in_call[call]], u_own, sems.at[2])

    def turn(slot):
        for k in range(STEP_BLOCKS):
            left = jnp.concatenate([ref[k] for ref in xr_refs], 0).T
            for ref, part in zip(lefts[slot], halves(left)):
                ref[k * B : (k + 1) * B, :] = part

    def multiply(slot):
        for top in range(0, STEP_BLOCKS * B, 256):
            left_high = lefts[slot][0][top : top + 256, :]
            left_low = lefts[slot][1][top : top + 256, :]
            for start in range(0, cols_here, 256):
                high = high_ref[:, start : start + 256]
                low = low_ref[:, start : start + 256]
                out_ref[top : top + 256, start : start + 256] = (
                    single(left_high, high) + single(left_high, low) + single(left_low, high)
                )

    @pl.when(step == 0)
    def _():
        m_copy().start()
        for piece in range(col_pieces):
            xc_copy(piece).start()
        for call in range(calls):

            @pl.when(chosen[call])
            def _(call=call):
                y_copy(call).start()

            @pl.when(chosen[call] & (row_index == col_index))
            def _(call=call):
                u_copy(call).start()

        row_ids, col_ids = example_ids(row_index, col_index)
        to_cols = jnp.where(row_ids == col_ids, 1.0, 0.0).astype(jnp.bfloat16)
        turn(0)
        m_copy().wait()
        m_high, m_low = [single(part, to_cols).astype(jnp.bfloat16) for part in halves(m_own[...])]
        for piece in range(col_pieces):
            xc_copy(piece).wait()
        for start in range(0, COL_BLOCKS, 2):
            columns = [jnp.concatenate([xc_own[piece, start + k] for piece in range(col_pieces)], 0) for k in range(2)]
            x_high, x_low = halves(jnp.concatenate(columns, 1))
            right = single(m_high, x_high) + single(m_high, x_low) + single(m_low, x_high)
            high, low = halves(right)
            high_ref[:, start * B : (start + 2) * B] = high
            low_ref[:, start * B : (start + 2) * B] = low

        for call in range(calls):

            @pl.when(chosen[call])
            def _(call=call):
                y_copy(call).wait()
                high, low = halves(y_own[...])
                high_ref[:, :B] = high
                low_ref[:, :B] = low

            @pl.when(chosen[call] & (row_index == col_index))
            def _(call=call):
                u_copy(call).wait()

    for slot in range(2):

        @pl.when((step > 0) & ((step + 1) % 2 == slot))
        def _(slot=slot):
            multiply(slot)
            turn(1 - slot)

    @pl.when((step > 0) & (row_index == col_index % N_ROW))
    def _():
        down = lax.broadcasted_iota(jnp.int32, (B, B), 0)
        along = lax.broadcasted_iota(jnp.int32, (B, B), 1)
        upper_half = col_index // N_ROW
        for k in range(STEP_BLOCKS // 2):
            block = (step - 1) * (STEP_BLOCKS // 2) + k
            rows = pl.ds(pl.multiple_of((2 * k + upper_half) * B, B), B)
            cols = pl.ds(pl.multiple_of(block * B, B), B)
            ridge = jnp.broadcast_to(damp_ref[pl.ds(col_index + N_COL * block, 1), :], (B, B))
            out_ref[rows, cols] = out_ref[rows, cols] + jnp.where(down == along, ridge, 0.0)

    @pl.when(step == 1)
    def _():
        product = out_ref[:B, :B]
        out_ref[:B, :] = jnp.zeros((B, cols_here), jnp.float32)

        @pl.when((col_index < PANEL_BLOCKS) & (row_index > col_index))
        def _():
            out_ref[:B, :B] = product

        @pl.when((col_index < PANEL_BLOCKS) & (row_index == col_index))
        def _():
            out_ref[:B, :B] = u_own[...].T


def tile(xr, xc, m, y, u, damp):
    rows_here, cols_here = ROW_BLOCKS * B, COL_BLOCKS * B
    steps = ROW_BLOCKS // STEP_BLOCKS
    held = [*xc, *y, *u, m]
    return pl.pallas_call(
        functools.partial(tile_kernel, len(xr), len(xc)),
        grid=(steps + 1,),
        in_specs=[
            pl.BlockSpec((STEP_BLOCKS,) + piece.shape[1:], lambda i: (jnp.minimum(i, steps - 1), 0, 0)) for piece in xr
        ]
        + [pl.BlockSpec(memory_space=pl.ANY)] * len(held)
        + [pl.BlockSpec(damp.shape, lambda i: (0, 0))],
        out_specs=pl.BlockSpec((STEP_BLOCKS * B, cols_here), lambda i: (jnp.maximum(i - 1, 0), 0)),
        scratch_shapes=[pltpu.VMEM((NEX, cols_here), jnp.bfloat16)] * 2
        + [
            pltpu.VMEM((len(xc),) + xc[0].shape, jnp.float32),
            pltpu.VMEM((NEX, NEX), jnp.float32),
            pltpu.VMEM((NEX, B), jnp.float32),
            pltpu.VMEM((B, B), jnp.float32),
            pltpu.SemaphoreType.DMA((3 + len(xc),)),
        ]
        + [pltpu.VMEM((STEP_BLOCKS * B, NEX), jnp.bfloat16)] * 4,
        out_shape=jax.ShapeDtypeStruct((rows_here, cols_here), jnp.float32),
        compiler_params=pltpu.CompilerParams(vmem_limit_bytes=TILE_VMEM),
        cost_estimate=pl.CostEstimate(flops=12_000_000_000, bytes_accessed=24_000_000, transcendentals=0),
        name="tile",
    )(*xr, *held, damp)


def moved(value, target):
    pairs = [(row * N_COL + col, target(row, col)) for row in range(N_ROW) for col in range(N_COL)]
    return lax.ppermute(value, ("row", "col"), pairs)


def swapped(value, mask):
    return moved(value, lambda row, col: row * N_COL + (col ^ mask))


def swapped_rows(value, mask):
    return moved(value, lambda row, col: (row ^ mask) * N_COL + col)


FAR, RING, CORE = 8, (2, 4, 6), 1
NEXT, LINE = 4, (1, 2, 3)


def shards(activations, out_grads, proj_act, proj_grad, damping):
    row_index = lax.axis_index("row")
    col_index = lax.axis_index("col")
    act_sketch = jnp.dot(activations, proj_act, preferred_element_type=jnp.float32)
    grad_sketch = jnp.dot(out_grads, proj_grad, preferred_element_type=jnp.float32)
    here = activations.shape[0] // TOK_EX
    sketches = jnp.einsum(
        "eti,etj->eij",
        act_sketch.reshape(here, TOK_EX, SA),
        grad_sketch.reshape(here, TOK_EX, SG),
        precision=PRECISE,
    ) * (TOK_EX * NEX) ** (-0.5)

    for_rows = sketches.reshape(here, ROW_BLOCKS, N_ROW, B).transpose(2, 1, 0, 3)
    for_panel = jnp.broadcast_to(
        sketches[:, :PANEL_BLOCKS].transpose(1, 0, 2), (N_ROW, PANEL_BLOCKS, here, B)
    )
    parcels = lax.all_to_all(jnp.concatenate([for_rows, for_panel], 1), "row", split_axis=0, concat_axis=0)
    group = N_ROW * here
    parcels = parcels.transpose(1, 0, 2, 3).reshape(ROW_BLOCKS + PANEL_BLOCKS, group, B)
    rows = parcels[:ROW_BLOCKS]
    panel = parcels[ROW_BLOCKS:]

    parity = col_index % 2
    split = rows.reshape(COL_BLOCKS, 2, group, B)
    near = lax.dynamic_index_in_dim(split, parity, 1, keepdims=False)
    other = lax.dynamic_index_in_dim(split, 1 - parity, 1, keepdims=False)
    tie = lax.optimization_barrier
    panel = jnp.concatenate([panel, swapped(panel, FAR)], 1)
    panels = [panel] + [swapped(panel, mask) for mask in RING]
    near = jnp.concatenate([near, swapped(other, CORE)], 1)
    panels, near, rows = tie((panels, near, rows))
    panels = panels + [swapped(piece, CORE) for piece in panels]
    cols = [
        moved(near, lambda row, col: (col // 2 ^ row ^ mask) * N_COL + row + N_ROW * (col % 2)) for mask in (0, NEXT)
    ]
    rows_far = swapped(rows, FAR)

    damp_blocks = damping.reshape(SA, B)
    m, y0, u0, square = chain(panels, damp_blocks, 0, None)
    m, cols, rows, rows_far = tie((m, cols, rows, rows_far))
    rows = jnp.concatenate([rows, rows_far], 1)
    pieces = [rows] + [swapped(rows, mask) for mask in RING]
    cols = jnp.concatenate(cols, 1)
    xc = [cols] + [swapped_rows(cols, mask) for mask in LINE]
    m, y1, u1, square = chain(panels, damp_blocks, 1, [m, square, y0])
    m, pieces = tie((m, pieces))
    pieces = pieces + [swapped(piece, CORE) for piece in pieces]
    m, y2, u2, square = chain(panels, damp_blocks, 2, [m, square, y1])
    return tile(pieces, xc, m, (y0, y1, y2), (u0, u1, u2), damp_blocks)


def solution(mesh):
    placed = (P(("row", "col"), None), P(("row", "col"), None), P(), P(), P())
    return jax.shard_map(
        shards, mesh=mesh, in_specs=placed, out_specs=P("row", "col"), check_vma=False
    )
```
